128 devices in a mesh: owner: 32 (over z, y, core), rep: 4 (over x).
Axes of the slice: x: 4, y: 4, z: 4, core: 2. Of those that a mesh axis runs over, the one named last changes fastest.
Arguments:
- paper_feat: bfloat16 [65536, 768], P('owner', 'rep'), may hold values from -6 to 6
- author_feat: bfloat16 [65536, 768], P('owner', 'rep'), may hold values from -6 to 6
- weights: bfloat16 [2, 768, 768], replicated, may hold values from -0.21875 to 0.21875
- relation: float32 [768], replicated, may hold values from -0.21875 to 0.21875
- send_rows: int32 [32, 32, 512], P('owner'), may hold values from 0 to 2047
- tile_src: int32 [1, 48, 512], P(None, None, 'owner'), may hold values from 0 to 127
- tile_col: int32 [1, 48, 65536], P(None, None, 'owner'), may hold values from 0 to 128, as said below
- cand_author: int32 [32768], P('owner'), may hold values from 0 to 2047
- cand_send: int32 [32, 32, 32], P('owner'), may hold values from 0 to 2047
- neg_rows: int32 [32, 32], P('owner'), may hold values from 0 to 2047
Outputs:
- refreshed: bfloat16 [65536, 768], P('owner', 'rep')
- edge_loss: float32 [32768], P('owner')
The draws below stay inside these ranges and needn't reach their ends.
Inputs may be any that keep to these rules, and one draw needn't show every extreme that they name: `tile_col`: entry 128 marks an empty slot; an author's live slots in a relation are its first ones, from none to 48 of them.
All inputs are finite; a program needn't handle non-finite values.
Results may differ from the reference program's by a relative error of at most 0.0065.
Values may be sent and summed in bfloat16 or wider, within the bound.
A program may use at most 64 MiB of HBM per device.

```python
import jax
import jax.numpy as jnp
from jax import lax

D = 768
R = 1
K_T = 48
CAP = 512
NEG_DEV = 32
A_DEV = 2048
P_DEV = 2048
E_DEV = 1024
AUTHORS = 65536
PAPERS = 65536
EDGES = 32768
NEG = 1024
RBLK = 128
ABLK = 512
CCAP = 32
N_OWNER = 32


def draw_tile_col(key, part):
    key = jax.random.fold_in(key, 11)
    key_degree, key_column = jax.random.split(key)
    degree = jax.random.randint(key_degree, (R, 1, AUTHORS), 0, K_T + 1)
    degree = degree.at[:, :, 0].set(0).at[:, :, 1].set(K_T)
    column = jax.random.randint(key_column, (R, K_T, AUTHORS), 0, 128)
    column = column.at[:, 0, 1].set(0)
    slots = lax.broadcasted_iota(jnp.int32, (R, K_T, AUTHORS), 1)
    return jnp.where(slots < degree, column, 128).astype(jnp.int32)


def set_ends(values, stream_key, low, high):
    longest = values.shape.index(max(values.shape))
    spots = []
    for shift in (0, 1):
        where = [jax.random.randint(jax.random.fold_in(stream_key, axis), (), 0, length) for axis, length in enumerate(values.shape)]
        where[longest] = (where[longest] + shift) % values.shape[longest]
        spots.append(tuple(where))
    return values.at[spots[0]].set(low).at[spots[1]].set(high)


def steps_of(key, extent, shards, smallest, largest):
    gain = 1.0
    for axis_at, blocks in shards:
        draws = jax.random.uniform(jax.random.fold_in(jax.random.fold_in(key, 6), axis_at), (blocks,), jnp.float32, smallest / len(shards), largest / len(shards))
        gain = gain * jnp.repeat(jnp.exp(draws), extent[axis_at] // blocks).reshape((-1,) + (1,) * (len(extent) - 1 - axis_at))
    return gain


def scatter_about(own_key, dims, deviation, limit, cuts=(), held_as=jnp.bfloat16):
    factor_of = steps_of(own_key, dims, cuts, -0.22, 0.18) if cuts else 1.0
    entries = jax.random.normal(own_key, dims, jnp.float32) * deviation * factor_of
    return jnp.minimum(jnp.maximum(entries, -limit), limit).astype(held_as)


def setup_inputs(seed: int = 0) -> dict:
    arg_keys = jax.random.split(jax.random.key(seed), 11)
    return {
        "paper_feat": scatter_about(arg_keys[0], (PAPERS, D), 1.0, 6.0, ((0, 32), (1, 4))),
        "author_feat": scatter_about(arg_keys[1], (AUTHORS, D), 1.0, 6.0, ((0, 32), (1, 4))),
        "weights": scatter_about(arg_keys[2], (R + 1, D, D), D ** -0.5, 0.21875),
        "relation": scatter_about(arg_keys[3], (D,), D ** -0.5, 0.21875, (), jnp.float32),
        "send_rows": set_ends(jax.random.randint(arg_keys[4], (N_OWNER, N_OWNER, CAP), 0, P_DEV), jax.random.fold_in(arg_keys[4], 1), 0, P_DEV - 1).astype(jnp.int32),
        "tile_src": set_ends(jax.random.randint(arg_keys[5], (R, K_T, ABLK), 0, RBLK), jax.random.fold_in(arg_keys[5], 1), 0, RBLK - 1).astype(jnp.int32),
        "tile_col": draw_tile_col(jax.random.fold_in(arg_keys[10], 71), 0),
        "cand_author": set_ends(jax.random.randint(arg_keys[7], (EDGES,), 0, A_DEV), jax.random.fold_in(arg_keys[7], 1), 0, A_DEV - 1).astype(jnp.int32),
        "cand_send": set_ends(jax.random.randint(arg_keys[8], (N_OWNER, N_OWNER, CCAP), 0, P_DEV), jax.random.fold_in(arg_keys[8], 1), 0, P_DEV - 1).astype(jnp.int32),
        "neg_rows": set_ends(jax.random.randint(arg_keys[9], (N_OWNER, NEG_DEV), 0, P_DEV), jax.random.fold_in(arg_keys[9], 1), 0, P_DEV - 1).astype(jnp.int32),
    }


def gather_rows(source, chosen):
    return jax.vmap(lambda a, b: jnp.take(a, b, axis=0))(source, chosen)


def reference(paper_feat, author_feat, weights, relation, send_rows, tile_src, tile_col, cand_author, cand_send, neg_rows):
    papers = paper_feat.reshape(N_OWNER, P_DEV, D)
    authors = author_feat.reshape(N_OWNER, A_DEV, D)
    negatives = gather_rows(papers, neg_rows).reshape(NEG, D)
    blocks_per = A_DEV // 128
    src_all = tile_src.reshape(R, K_T, N_OWNER, blocks_per).transpose(2, 0, 1, 3)
    col_all = tile_col.reshape(R, K_T, N_OWNER, A_DEV).transpose(2, 0, 1, 3)
    endpoint = cand_author.reshape(N_OWNER, E_DEV)

    def per_owner(owner_id):
        received = gather_rows(papers, send_rows[:, owner_id, :]).reshape(N_OWNER * CAP, D)
        block_of = jnp.repeat(src_all[owner_id], 128, axis=2)
        columns = col_all[owner_id]
        is_live = columns < 128
        row_index = (block_of * 128 + jnp.where(is_live, columns, 0)).astype(jnp.int32)

        def add_tile(summed, slot):
            picked = jnp.take(received, row_index[:, slot], axis=0).astype(jnp.float32)
            return summed + jnp.where(is_live[:, slot, :, None], picked, jnp.float32(0.0)), None

        summed, _ = lax.scan(add_tile, jnp.zeros((R, A_DEV, D), jnp.float32), jnp.arange(K_T, dtype=jnp.int32))
        counted = jnp.sum(is_live.astype(jnp.float32), axis=1)
        averages = (summed / jnp.maximum(counted, 1.0)[..., None]).astype(jnp.bfloat16)
        mixed = jnp.dot(authors[owner_id], weights[0], preferred_element_type=jnp.float32)
        for rel_id in range(R):
            mixed = mixed + jnp.dot(averages[rel_id], weights[1 + rel_id], preferred_element_type=jnp.float32)
        refreshed = mixed.astype(jnp.bfloat16)
        cand_rows = gather_rows(papers, cand_send[:, owner_id, :]).reshape(E_DEV, D)
        queries = (jnp.take(refreshed, endpoint[owner_id], axis=0).astype(jnp.float32) * relation).astype(jnp.bfloat16)
        positive = jnp.sum(queries.astype(jnp.float32) * cand_rows.astype(jnp.float32), axis=1)
        negative = jnp.dot(queries, negatives.T, preferred_element_type=jnp.float32)
        losses = jax.nn.softplus(-positive) + jnp.mean(jax.nn.softplus(negative), axis=1)
        return refreshed, losses

    refreshed, losses = lax.map(per_owner, jnp.arange(N_OWNER, dtype=jnp.int32))
    return refreshed.reshape(AUTHORS, D), losses.reshape(EDGES)
```

```python
import jax
import jax.numpy as jnp
from jax import lax
from jax.experimental import pallas as pl
from jax.experimental.pallas import tpu as pltpu
from jax.sharding import PartitionSpec as P

MESH = pl.DeviceIdType.MESH
BF = jnp.bfloat16
F32 = jnp.float32
I32 = jnp.int32

W = 192
ROWS = 2048
CAP = 512
SLOTS = 48
D = 768


def iota(shape, dim):
    return lax.broadcasted_iota(I32, shape, dim)


def one_hot(rows, picks):
    return (iota((rows, picks.shape[1]), 0) == picks).astype(BF)


def kernel(
    src_ref,
    paper_ref,
    author_ref,
    weights_ref,
    relation_ref,
    idx_ref,
    col_ref,
    edge_ref,
    out_ref,
    loss_ref,
    paper_t,
    author_t,
    idx_all,
    send_buf,
    recv,
    cand_acc,
    neg_acc,
    cand_send,
    neg_send,
    cand_rx,
    cand_all,
    neg_all,
    neg_rows,
    weights_v,
    weights_t,
    relation_b,
    avg_all,
    self_part,
    self_sel,
    avg_sel,
    edge_hot,
    w_sem,
    p1_send,
    p1_recv,
    i1_send,
    i1_recv,
    au_send,
    au_recv,
    main_send,
    main_recv,
    cand_ssem,
    cand_rsem,
    neg_ssem,
    neg_rsem,
    nx_send,
    nx_recv,
    swap_send,
    swap_recv,
    cx_send,
    cx_recv,
    avg_ssem,
    avg_rsem,
    loss_ssem,
    loss_rsem,
):
    owner = lax.axis_index("owner")
    x = lax.axis_index("rep")
    core = owner % 2
    y = (owner // 2) % 4
    z = owner // 8
    even = 1 - core
    a = z * even + y * core
    b = y * even + z * core

    def owner_at(a_pos, b_pos, core_pos):
        return (a_pos * even + b_pos * core) * 8 + (b_pos * even + a_pos * core) * 2 + core_pos

    def device(da=0, db=0, dcore=0, dx=0):
        return {
            "owner": owner_at((a + da) % 4, (b + db) % 4, (core + dcore) % 2),
            "rep": (x + dx) % 4,
        }

    def remote(src, dst, ssem, rsem, target):
        return pltpu.make_async_remote_copy(
            src_ref=src,
            dst_ref=dst,
            send_sem=ssem,
            recv_sem=rsem,
            device_id=target,
            device_id_type=MESH,
        )

    barrier = pltpu.get_barrier_semaphore()
    partners = [device(da=k) for k in (1, 2, 3)] + [device(db=k) for k in (1, 2, 3)]
    partners += [device(da=k, dcore=1) for k in (0, 1, 2, 3)]
    partners += [device(db=k, dcore=1) for k in (1, 2, 3)]
    partners += [device(dx=k) for k in (1, 2, 3)]
    for partner in partners:
        pl.semaphore_signal(barrier, inc=1, device_id=partner, device_id_type=MESH)

    weights_copy = pltpu.make_async_copy(weights_ref, weights_v, w_sem)
    weights_copy.start()
    paper_t[0] = jnp.transpose(paper_ref[...])
    author_t[x] = jnp.transpose(author_ref[...])
    idx_all[0] = idx_ref[a]
    pl.semaphore_wait(barrier, len(partners))

    first = []
    for da in (1, 3, 2):
        slot = 4 - da
        first.append(
            remote(
                idx_ref.at[(a + da) % 4], idx_all.at[slot], i1_send.at[slot], i1_recv.at[slot], device(da=da)
            )
        )
        first.append(
            remote(paper_t.at[0], paper_t.at[slot], p1_send.at[slot], p1_recv.at[slot], device(da=da))
        )
    for copy in first:
        copy.start()
    authors = []
    for dx in (1, 3, 2):
        authors.append(
            remote(author_t.at[x], author_t.at[x], au_send.at[dx], au_recv.at[dx], device(dx=dx))
        )
    for copy in authors:
        copy.start()

    def main_copy(da, k):
        db = (k // 2 + 1) % 4
        dcore = k % 2
        source = owner_at((a + da) % 4, b, core)
        return remote(
            send_buf.at[da, k],
            recv.at[pl.ds(4 * source, 4)],
            main_send.at[da, k],
            main_recv.at[source],
            device(db=db, dcore=dcore),
        )

    def main_local(da, k):
        source = owner_at((a + da) % 4, b, core)
        return pltpu.make_async_copy(
            send_buf.at[da, k], recv.at[pl.ds(4 * source, 4)], main_recv.at[source]
        )

    def select_main(da):
        def step(k, carry):
            row = ((b + k // 2 + 1) % 4) * 2 + (core + k) % 2
            picks = idx_all[da, pl.ds(row, 1), :]
            out = jnp.dot(paper_t[da], one_hot(ROWS, picks), preferred_element_type=F32).astype(BF)
            for j in range(4):
                send_buf[da, k, j] = out[:, j * 128 : (j + 1) * 128]

            @pl.when(k == 6)
            def _():
                main_local(da, k).start()

            @pl.when(k != 6)
            def _():
                main_copy(da, k).start()

            return carry

        lax.fori_loop(0, 8, step, 0)

    group = iota((W, 128), 1) // 32

    def select_extra(da):
        a_src = (a + da) % 4
        picks = idx_all[da, 8:9, 0:384]
        out = jnp.dot(paper_t[da], one_hot(ROWS, picks), preferred_element_type=F32)
        here = group == a_src
        for d in range(8):
            part = out[:, (d // 4) * 128 : (d // 4 + 1) * 128]
            part = pltpu.roll(part, ((a_src + 4 - d % 4) % 4) * 32, 1)
            old = jnp.zeros((W, 128), F32) if da == 0 else cand_acc[d]
            cand_acc[d] = jnp.where(here, part, old)
        old = jnp.zeros((W, 128), F32) if da == 0 else neg_acc[...]
        neg_acc[...] = jnp.where(here, out[:, 256:384], old)

    def cand_copy(k):
        return remote(
            cand_send.at[((b + k // 2 + 1) % 4) * 2 + (core + k) % 2],
            cand_rx.at[b, core],
            cand_ssem.at[k],
            cand_rsem.at[b * 2 + core],
            device(db=(k // 2 + 1) % 4, dcore=k % 2),
        )

    def cand_local():
        return pltpu.make_async_copy(
            cand_send.at[b * 2 + core], cand_rx.at[b, core], cand_rsem.at[b * 2 + core]
        )

    def neg_copy(db):
        return remote(
            neg_send, neg_all.at[core, x, b], neg_ssem.at[db], neg_rsem.at[b], device(db=db)
        )

    def neg_local():
        return pltpu.make_async_copy(neg_send, neg_all.at[core, x, b], neg_rsem.at[b])

    select_main(0)
    select_extra(0)
    weights_copy.wait()
    for w in range(2):
        weights_t[w] = jnp.transpose(weights_v[w])
    for i in range(6):
        row = jnp.broadcast_to(relation_ref[i : i + 1, :], (128, 128))
        relation_b[pl.ds(i * 128, 128), :] = jnp.transpose(row)
    edge_hot[...] = one_hot(ROWS, edge_ref[...])

    def first_wait(slot):
        first_idx = remote(
            idx_ref.at[0], idx_all.at[slot], i1_send.at[slot], i1_recv.at[slot], device(da=1)
        )
        first_paper = remote(
            paper_t.at[0], paper_t.at[slot], p1_send.at[slot], p1_recv.at[slot], device(da=1)
        )
        first_idx.wait_recv()
        first_paper.wait_recv()

    first_wait(1)
    select_extra(1)
    select_main(1)
    first_wait(3)
    select_extra(3)
    first_wait(2)
    select_extra(2)
    for d in range(8):
        cand_send[d] = cand_acc[d].astype(BF)
    neg_send[...] = neg_acc[...].astype(BF)
    for db in (1, 3, 2):
        neg_copy(db).start()
    neg_local().start()
    for k in (0, 1, 2, 3, 4, 5, 7):
        cand_copy(k).start()
    cand_local().start()
    select_main(3)

    for slot in range(4):
        pltpu.make_async_copy(neg_send, neg_all.at[core, x, slot], neg_rsem.at[slot]).wait()
    neg_x = [
        remote(neg_all.at[core, x], neg_all.at[core, x], nx_send.at[dx], nx_recv.at[dx], device(dx=dx))
        for dx in (1, 3, 2)
    ]
    for copy in neg_x:
        copy.start()
    for slot in range(8):
        pltpu.make_async_copy(
            cand_send.at[0], cand_rx.at[slot // 2, slot % 2], cand_rsem.at[slot]
        ).wait()
    cand_x = [
        remote(
            cand_rx.at[(x + dx) % 4], cand_all.at[x], cx_send.at[dx], cx_recv.at[dx], device(dx=dx)
        )
        for dx in (1, 3, 2)
    ]
    for copy in cand_x:
        copy.start()
    cand_all[x] = cand_rx[x]
    select_main(2)

    for copy in neg_x:
        copy.wait_recv()
    swap = remote(neg_all.at[core], neg_all.at[core], swap_send, swap_recv, device(dcore=1))
    swap.start()

    for copy in authors:
        copy.wait_recv()
    own_rows = pl.ds(pl.multiple_of(x * W, 16), W)
    for g in range(4):
        lanes = pl.ds(g * 512, 512)
        block = jnp.concatenate([author_t[i, :, lanes] for i in range(4)], axis=0)
        self_part[:, lanes] = jnp.dot(weights_t[0, own_rows, :], block, preferred_element_type=F32)
    author_sel = [
        jnp.dot(author_t[i], edge_hot[...], preferred_element_type=F32).astype(BF) for i in range(4)
    ]
    self_sel[...] = jnp.dot(
        weights_t[0], jnp.concatenate(author_sel, axis=0), preferred_element_type=F32
    )
    swap.wait()
    for c in range(2):
        for i in range(4):
            block = jnp.concatenate([neg_all[c, j, i] for j in range(4)], axis=0)
            neg_rows[pl.ds((c * 4 + i) * 128, 128), :] = jnp.transpose(block)

    def recv_wait(s, carry):
        pltpu.make_async_copy(
            send_buf.at[0, 0], recv.at[pl.ds(4 * s, 4)], main_recv.at[s]
        ).wait()
        return carry

    lax.fori_loop(0, 32, recv_wait, 0)

    def avg_copy(g, dx):
        return remote(
            avg_all.at[x, g], avg_all.at[x, g], avg_ssem.at[g, dx], avg_rsem.at[g, dx], device(dx=dx)
        )

    def aggregate(block, carry):
        lanes = pl.ds(pl.multiple_of(block * 128, 128), 128)
        live = (col_ref[:, lanes] < 128).astype(F32)
        scale = 1.0 / jnp.maximum(jnp.sum(live, axis=0, keepdims=True), 1.0)
        total = jnp.zeros((W, 128), F32)
        for t in range(0, SLOTS, 8):
            left = [recv[src_ref[t + i, block]] for i in range(8)]
            right = [one_hot(128, col_ref[t + i : t + i + 1, lanes]) for i in range(8)]
            total = total + jnp.dot(
                jnp.concatenate(left, axis=1),
                jnp.concatenate(right, axis=0),
                preferred_element_type=F32,
            )
        g = block // 4
        inner = pl.ds(pl.multiple_of((block % 4) * 128, 128), 128)
        avg_all[x, g, :, inner] = (total * scale).astype(BF)

        @pl.when(block % 4 == 3)
        def _():
            for dx in (1, 3, 2):
                avg_copy(g, dx).start()

        return carry

    lax.fori_loop(0, 16, aggregate, 0)

    avg_sel[...] = jnp.zeros_like(avg_sel)

    def dense(g, carry):
        for dx in (1, 3, 2):
            avg_copy(g, dx).wait_recv()
        lanes = pl.ds(pl.multiple_of(g * 512, 512), 512)
        block = jnp.concatenate([avg_all[i, g] for i in range(4)], axis=0)
        mixed = self_part[:, lanes] + jnp.dot(
            weights_t[1, own_rows, :], block, preferred_element_type=F32
        )
        out_ref[:, lanes] = mixed.astype(BF)
        hot = edge_hot[pl.ds(pl.multiple_of(g * 512, 512), 512), :]
        avg_sel[...] += jnp.dot(block, hot, preferred_element_type=F32)
        return carry

    lax.fori_loop(0, 4, dense, 0)

    refreshed = self_sel[...] + jnp.dot(
        weights_t[1], avg_sel[...].astype(BF), preferred_element_type=F32
    )
    gain = jnp.concatenate([relation_b[...]] * 2, axis=1)
    queries = (refreshed.astype(BF).astype(F32) * gain).astype(BF)
    for copy in cand_x:
        copy.wait_recv()
    positive = jnp.zeros((1, 256), F32)
    for i in range(4):
        rows = jnp.concatenate([cand_all[i, 0], cand_all[i, 1]], axis=1).astype(F32)
        query = queries[i * W : (i + 1) * W].astype(F32)
        positive = positive + jnp.sum(query * rows, axis=0, keepdims=True)

    def softplus(v):
        return jnp.maximum(v, 0.0) + jnp.log1p(jnp.exp(-jnp.abs(v)))

    negative = jnp.dot(neg_rows[...], queries, preferred_element_type=F32)
    losses = softplus(-positive) + jnp.sum(softplus(negative), axis=0, keepdims=True) / 1024.0
    loss_ref[x, 0:1, :] = losses[:, 0:128]
    loss_ref[x, 1:2, :] = losses[:, 128:256]
    loss_copies = [
        remote(loss_ref.at[x], loss_ref.at[x], loss_ssem.at[dx], loss_rsem.at[dx], device(dx=dx))
        for dx in (1, 3, 2)
    ]
    for copy in loss_copies:
        copy.start()

    for copy in first + authors + neg_x + cand_x:
        copy.wait_send()
    for db in (1, 3, 2):
        neg_copy(db).wait_send()
    for k in (0, 1, 2, 3, 4, 5, 7):
        cand_copy(k).wait_send()

    def main_drain(k, carry):
        for da in range(4):

            @pl.when(k != 6)
            def _():
                main_copy(da, k).wait_send()

        return carry

    lax.fori_loop(0, 8, main_drain, 0)
    for g in range(4):
        for dx in (1, 3, 2):
            avg_copy(g, dx).wait_send()
    for copy in loss_copies:
        copy.wait()


def per_device(
    paper_feat,
    author_feat,
    weights,
    relation,
    send_rows,
    tile_src,
    tile_col,
    cand_author,
    cand_send,
    neg_rows,
):
    core = lax.axis_index("owner") % 2
    x = lax.axis_index("rep")

    def by_a(lists):
        lists = lists[0].reshape(4, 4, 2, -1)
        return jnp.where(core == 1, lists.transpose(1, 0, 2, 3), lists)

    rows = by_a(send_rows).reshape(4, 8, CAP)
    cands = by_a(cand_send).reshape(4, 1, 256)
    negs = jnp.broadcast_to(jnp.tile(neg_rows, (1, 4))[None], (4, 1, 128))
    last = jnp.concatenate([cands, negs, jnp.zeros((4, 1, 128), I32)], axis=2)
    idx = jnp.concatenate([rows, last, jnp.zeros((4, 7, CAP), I32)], axis=1)
    grid = cand_author.reshape(4, 4, 2, 32)
    first = lax.dynamic_index_in_dim(grid[:, :, 0], x, 1, keepdims=False).reshape(1, 128)
    second = lax.dynamic_index_in_dim(grid[:, :, 1], x, 0, keepdims=False).reshape(1, 128)
    edges = jnp.concatenate([first, second], axis=1)

    vmem = pl.BlockSpec(memory_space=pltpu.VMEM)
    dma = pltpu.SemaphoreType.DMA
    out, loss = pl.pallas_call(
        kernel,
        out_shape=(
            jax.ShapeDtypeStruct((W, ROWS), BF),
            jax.ShapeDtypeStruct((4, 8, 128), F32),
        ),
        in_specs=[
            pl.BlockSpec(memory_space=pltpu.SMEM),
            vmem,
            vmem,
            pl.BlockSpec(memory_space=pl.ANY),
            vmem,
            vmem,
            vmem,
            vmem,
        ],
        out_specs=(vmem, vmem),
        scratch_shapes=[
            pltpu.VMEM((4, W, ROWS), BF),
            pltpu.VMEM((4, W, ROWS), BF),
            pltpu.VMEM((4, 16, CAP), I32),
            pltpu.VMEM((4, 8, 4, W, 128), BF),
            pltpu.VMEM((128, W, 128), BF),
            pltpu.VMEM((8, W, 128), F32),
            pltpu.VMEM((W, 128), F32),
            pltpu.VMEM((8, W, 128), BF),
            pltpu.VMEM((W, 128), BF),
            pltpu.VMEM((4, 2, W, 128), BF),
            pltpu.VMEM((4, 2, W, 128), BF),
            pltpu.VMEM((2, 4, 4, W, 128), BF),
            pltpu.VMEM((1024, D), BF),
            pltpu.VMEM((2, D, D), BF),
            pltpu.VMEM((2, D, D), BF),
            pltpu.VMEM((D, 128), F32),
            pltpu.VMEM((4, 4, W, 512), BF),
            pltpu.VMEM((W, ROWS), F32),
            pltpu.VMEM((D, 256), F32),
            pltpu.VMEM((D, 256), F32),
            pltpu.VMEM((ROWS, 256), BF),
            dma,
            dma((4,)),
            dma((4,)),
            dma((4,)),
            dma((4,)),
            dma((4,)),
            dma((4,)),
            dma((4, 8)),
            dma((32,)),
            dma((8,)),
            dma((8,)),
            dma((4,)),
            dma((4,)),
            dma((4,)),
            dma((4,)),
            dma,
            dma,
            dma((4,)),
            dma((4,)),
            dma((4, 4)),
            dma((4, 4)),
            dma((4,)),
            dma((4,)),
        ],
        compiler_params=pltpu.CompilerParams(
            collective_id=0, has_side_effects=True, vmem_limit_bytes=60 * 2**20
        ),
        name="conv_and_score",
    )(
        tile_src[0],
        paper_feat,
        author_feat,
        weights,
        relation.reshape(6, 128),
        idx,
        tile_col[0],
        edges,
    )
    refreshed = out.T
    even = loss[:, 0].reshape(4, 4, 32).transpose(1, 0, 2)
    odd = loss[:, 1].reshape(4, 4, 32)
    return refreshed, jnp.stack([even, odd], axis=2).reshape(-1)


def solution(mesh):
    placed = (
        P("owner", "rep"),
        P("owner", "rep"),
        P(),
        P(),
        P("owner", None, None),
        P(None, None, "owner"),
        P(None, None, "owner"),
        P("owner"),
        P("owner", None, None),
        P("owner", None),
    )
    return jax.shard_map(
        per_device,
        mesh=mesh,
        in_specs=placed,
        out_specs=(P("owner", "rep"), P("owner")),
        check_vma=False,
    )
```

```python
import jax
import jax.numpy as jnp
from jax import lax
from jax.experimental import pallas as pl
from jax.experimental.pallas import tpu as pltpu
from jax.sharding import PartitionSpec as P

MESH = pl.DeviceIdType.MESH
BF = jnp.bfloat16
F32 = jnp.float32
I32 = jnp.int32

W = 192
ROWS = 2048
CAP = 512
HALF = 96
SLOTS = 48
D = 768


def iota(shape, dim):
    return lax.broadcasted_iota(I32, shape, dim)


def one_hot(rows, picks):
    return (iota((rows, picks.shape[1]), 0) == picks).astype(BF)


def kernel(
    src_ref,
    paper_ref,
    author_ref,
    weights_ref,
    relation_ref,
    idx_ref,
    col_ref,
    edge_ref,
    out_ref,
    loss_ref,
    paper_t,
    author_t,
    idx_all,
    send_buf,
    recv_first,
    recv_second,
    cand_acc,
    neg_acc,
    cand_send,
    neg_send,
    cand_rx,
    cand_all,
    neg_all,
    neg_rows,
    weights_v,
    weights_t,
    relation_b,
    avg_all,
    self_part,
    self_sel,
    avg_sel,
    edge_hot,
    w_sem,
    p1_send,
    p1_recv,
    f1_send,
    f1_recv,
    i1_send,
    i1_recv,
    au_send,
    au_recv,
    fa_send,
    fa_recv,
    main_send,
    main_recv,
    cand_ssem,
    cand_rsem,
    neg_ssem,
    neg_rsem,
    nx_send,
    nx_recv,
    swap_send,
    swap_recv,
    cx_send,
    cx_recv,
    avg_ssem,
    avg_rsem,
    fw_ssem,
    fw_rsem,
    loss_ssem,
    loss_rsem,
):
    recv = (recv_first, recv_second)
    owner = lax.axis_index("owner")
    x = lax.axis_index("rep")
    core = owner % 2
    y = (owner // 2) % 4
    z = owner // 8
    even = 1 - core
    a = z * even + y * core
    b = y * even + z * core

    def owner_at(a_pos, b_pos, core_pos):
        return (a_pos * even + b_pos * core) * 8 + (b_pos * even + a_pos * core) * 2 + core_pos

    def device(da=0, db=0, dcore=0, dx=0):
        return {
            "owner": owner_at((a + da) % 4, (b + db) % 4, (core + dcore) % 2),
            "rep": (x + dx) % 4,
        }

    def remote(src, dst, ssem, rsem, target):
        return pltpu.make_async_remote_copy(
            src_ref=src,
            dst_ref=dst,
            send_sem=ssem,
            recv_sem=rsem,
            device_id=target,
            device_id_type=MESH,
        )

    barrier = pltpu.get_barrier_semaphore()
    partners = [device(da=k) for k in (1, 2, 3)] + [device(db=k) for k in (1, 2, 3)]
    partners += [device(da=k, dcore=1) for k in (0, 1, 2, 3)]
    partners += [device(db=k, dcore=1) for k in (1, 2, 3)]
    partners += [device(dx=k) for k in (1, 2, 3)]
    for partner in partners:
        pl.semaphore_signal(barrier, inc=1, device_id=partner, device_id_type=MESH)

    weights_copy = pltpu.make_async_copy(weights_ref, weights_v, w_sem)
    weights_copy.start()
    paper_t[0] = jnp.transpose(paper_ref[...])
    author_t[x] = jnp.transpose(author_ref[...])
    idx_all[0] = idx_ref[a]
    pl.semaphore_wait(barrier, len(partners))

    def row_list(da):
        slot = 4 - da
        return remote(
            idx_ref.at[(a + da) % 4], idx_all.at[slot], i1_send.at[slot], i1_recv.at[slot], device(da=da)
        )

    def paper_copy(da):
        slot = 4 - da
        return remote(
            paper_t.at[0], paper_t.at[slot], p1_send.at[slot], p1_recv.at[slot], device(da=da)
        )

    def half_of(way):
        return pl.ds(0 if way == 1 else HALF, HALF)

    def paper_forward(da):
        slot = 4 - da
        return remote(
            paper_t.at[slot, half_of(da)],
            paper_t.at[2, half_of(da)],
            f1_send.at[slot],
            f1_recv.at[slot],
            device(da=da),
        )

    def author_copy(dx):
        return remote(author_t.at[x], author_t.at[x], au_send.at[dx], au_recv.at[dx], device(dx=dx))

    def author_forward(dx):
        part = author_t.at[(x + 4 - dx) % 4, half_of(dx)]
        return remote(part, part, fa_send.at[dx], fa_recv.at[dx], device(dx=dx))

    for da in (1, 3, 2):
        row_list(da).start()
    for da in (1, 3):
        paper_copy(da).start()
    for dx in (1, 3):
        author_copy(dx).start()

    def main_copy(da, k, h):
        db = (k // 2 + 1) % 4
        dcore = k % 2
        source = owner_at((a + da) % 4, b, core)
        return remote(
            send_buf.at[da, k, h],
            recv[h].at[pl.ds(4 * source, 4)],
            main_send.at[h, da, k],
            main_recv.at[h, source],
            device(db=db, dcore=dcore),
        )

    def main_start(da, k, h):
        @pl.when(k == 6)
        def _():
            source = owner_at((a + da) % 4, b, core)
            pltpu.make_async_copy(
                send_buf.at[da, k, h], recv[h].at[pl.ds(4 * source, 4)], main_recv.at[h, source]
            ).start()

        @pl.when(k != 6)
        def _():
            main_copy(da, k, h).start()

    def select_main(da):
        def step(k, carry):
            row = ((b + k // 2 + 1) % 4) * 2 + (core + k) % 2
            picks = idx_all[da, pl.ds(row, 1), :]
            out = jnp.dot(paper_t[da], one_hot(ROWS, picks), preferred_element_type=F32).astype(BF)
            for h in range(2):
                for j in range(4):
                    send_buf[da, k, h, j] = out[h * HALF : (h + 1) * HALF, j * 128 : (j + 1) * 128]
            main_start(da, k, 0)
            return carry

        lax.fori_loop(0, 8, step, 0)

    group = iota((W, 128), 1) // 32

    def select_extra(da):
        a_src = (a + da) % 4
        picks = idx_all[da, 8:9, 0:384]
        out = jnp.dot(paper_t[da], one_hot(ROWS, picks), preferred_element_type=F32)
        here = group == a_src
        for d in range(8):
            part = out[:, (d // 4) * 128 : (d // 4 + 1) * 128]
            part = pltpu.roll(part, ((a_src + 4 - d % 4) % 4) * 32, 1)
            old = jnp.zeros((W, 128), F32) if da == 0 else cand_acc[d]
            cand_acc[d] = jnp.where(here, part, old)
        old = jnp.zeros((W, 128), F32) if da == 0 else neg_acc[...]
        neg_acc[...] = jnp.where(here, out[:, 256:384], old)

    def cand_copy(k):
        return remote(
            cand_send.at[((b + k // 2 + 1) % 4) * 2 + (core + k) % 2],
            cand_rx.at[b, core],
            cand_ssem.at[k],
            cand_rsem.at[b * 2 + core],
            device(db=(k // 2 + 1) % 4, dcore=k % 2),
        )

    def cand_local():
        return pltpu.make_async_copy(
            cand_send.at[b * 2 + core], cand_rx.at[b, core], cand_rsem.at[b * 2 + core]
        )

    def neg_copy(db):
        return remote(
            neg_send, neg_all.at[core, x, b], neg_ssem.at[db], neg_rsem.at[b], device(db=db)
        )

    def neg_local():
        return pltpu.make_async_copy(neg_send, neg_all.at[core, x, b], neg_rsem.at[b])

    select_main(0)
    select_extra(0)
    weights_copy.wait()
    for w in range(2):
        for h in range(2):
            rows = [weights_v[w, pl.ds(i * W + h * HALF, HALF), :] for i in range(4)]
            weights_t[w, h] = jnp.transpose(jnp.concatenate(rows, axis=0))
    for i in range(6):
        row = jnp.broadcast_to(relation_ref[i : i + 1, :], (128, 128))
        relation_b[pl.ds(i * 128, 128), :] = jnp.transpose(row)
    edge_hot[...] = one_hot(ROWS, edge_ref[...])

    for da in (1, 3):
        paper_copy(da).wait_recv()
        paper_forward(da).start()
    row_list(3).wait_recv()
    select_main(1)
    select_extra(1)
    row_list(1).wait_recv()
    select_main(3)
    select_extra(3)
    for dx in (1, 3):
        author_copy(dx).wait_recv()
        author_forward(dx).start()
    row_list(2).wait_recv()
    for da in (1, 3):
        paper_forward(da).wait_recv()
    select_extra(2)
    for d in range(8):
        cand_send[d] = cand_acc[d].astype(BF)
    neg_send[...] = neg_acc[...].astype(BF)
    for db in (1, 3, 2):
        neg_copy(db).start()
    neg_local().start()
    for k in (0, 1, 2, 3, 4, 5, 7):
        cand_copy(k).start()
    cand_local().start()
    select_main(2)

    def second_half(k, carry):
        for da in (0, 1, 3, 2):
            main_start(da, k, 1)
        return carry

    lax.fori_loop(0, 8, second_half, 0)

    for slot in range(4):
        pltpu.make_async_copy(neg_send, neg_all.at[core, x, slot], neg_rsem.at[slot]).wait()
    neg_x = [
        remote(neg_all.at[core, x], neg_all.at[core, x], nx_send.at[dx], nx_recv.at[dx], device(dx=dx))
        for dx in (1, 3, 2)
    ]
    for copy in neg_x:
        copy.start()
    for slot in range(8):
        pltpu.make_async_copy(
            cand_send.at[0], cand_rx.at[slot // 2, slot % 2], cand_rsem.at[slot]
        ).wait()
    cand_x = [
        remote(
            cand_rx.at[(x + dx) % 4], cand_all.at[x], cx_send.at[dx], cx_recv.at[dx], device(dx=dx)
        )
        for dx in (1, 3, 2)
    ]
    for copy in cand_x:
        copy.start()
    cand_all[x] = cand_rx[x]

    def avg_copy(h, g, dx):
        part = avg_all.at[h, x, g]
        return remote(part, part, avg_ssem.at[h, g, dx], avg_rsem.at[h, g, dx], device(dx=dx))

    def avg_forward(h, g, dx):
        part = avg_all.at[h, (x + 4 - dx) % 4, g, pl.ds(0 if dx == 1 else HALF // 2, HALF // 2)]
        return remote(part, part, fw_ssem.at[h, g, dx], fw_rsem.at[h, g, dx], device(dx=dx))

    def pass_on(h, g):
        for dx in (1, 3):
            avg_copy(h, g, dx).wait_recv()
            avg_forward(h, g, dx).start()

    def aggregate(h):
        def recv_wait(s, carry):
            pltpu.make_async_copy(
                send_buf.at[0, 0, h], recv[h].at[pl.ds(4 * s, 4)], main_recv.at[h, s]
            ).wait()
            return carry

        lax.fori_loop(0, 32, recv_wait, 0)

        def step(block, carry):
            lanes = pl.ds(pl.multiple_of(block * 128, 128), 128)
            live = (col_ref[:, lanes] < 128).astype(F32)
            scale = 1.0 / jnp.maximum(jnp.sum(live, axis=0, keepdims=True), 1.0)
            total = jnp.zeros((HALF, 128), F32)
            for t in range(0, SLOTS, 8):
                left = [recv[h][src_ref[t + i, block]] for i in range(8)]
                right = [one_hot(128, col_ref[t + i : t + i + 1, lanes]) for i in range(8)]
                total = total + jnp.dot(
                    jnp.concatenate(left, axis=1),
                    jnp.concatenate(right, axis=0),
                    preferred_element_type=F32,
                )
            g = block // 4
            inner = pl.ds(pl.multiple_of((block % 4) * 128, 128), 128)
            avg_all[h, x, g, :, inner] = (total * scale).astype(BF)

            @pl.when(block % 4 == 3)
            def _():
                for dx in (1, 3):
                    avg_copy(h, g, dx).start()

            @pl.when(block % 4 == 3)
            def _():
                @pl.when(g >= 2)
                def _():
                    pass_on(h, g - 2)

            return carry

        lax.fori_loop(0, 16, step, 0)

    aggregate(0)

    own_rows = pl.ds(pl.multiple_of(x * W, 16), W)
    pass_on(0, 2)
    for dx in (1, 3):
        author_forward(dx).wait_recv()
    for g in range(4):
        lanes = pl.ds(g * 512, 512)
        total = jnp.zeros((W, 512), F32)
        for h in range(2):
            block = [author_t[i, pl.ds(h * HALF, HALF), lanes] for i in range(4)]
            total = total + jnp.dot(
                weights_t[0, h, own_rows, :],
                jnp.concatenate(block, axis=0),
                preferred_element_type=F32,
            )
        self_part[:, lanes] = total
    pass_on(0, 3)
    author_sel = [
        jnp.dot(author_t[i], edge_hot[...], preferred_element_type=F32).astype(BF) for i in range(4)
    ]
    total = jnp.zeros((D, 256), F32)
    for h in range(2):
        block = [author_sel[i][h * HALF : (h + 1) * HALF] for i in range(4)]
        total = total + jnp.dot(
            weights_t[0, h], jnp.concatenate(block, axis=0), preferred_element_type=F32
        )
    self_sel[...] = total
    for copy in neg_x:
        copy.wait_recv()
    swap = remote(neg_all.at[core], neg_all.at[core], swap_send, swap_recv, device(dcore=1))
    swap.start()
    swap.wait()
    for c in range(2):
        for i in range(4):
            block = jnp.concatenate([neg_all[c, j, i] for j in range(4)], axis=0)
            neg_rows[pl.ds((c * 4 + i) * 128, 128), :] = jnp.transpose(block)

    aggregate(1)
    pass_on(1, 2)

    def dense(h):
        avg_sel[...] = jnp.zeros_like(avg_sel)

        def step(g, carry):
            for dx in (1, 3):
                avg_forward(h, g, dx).wait_recv()
            lanes = pl.ds(pl.multiple_of(g * 512, 512), 512)
            block = jnp.concatenate([avg_all[h, i, g] for i in range(4)], axis=0)
            mixed = self_part[:, lanes] + jnp.dot(
                weights_t[1, h, own_rows, :], block, preferred_element_type=F32
            )
            if h == 0:
                self_part[:, lanes] = mixed
            else:
                out_ref[:, lanes] = mixed.astype(BF)
            hot = edge_hot[pl.ds(pl.multiple_of(g * 512, 512), 512), :]
            avg_sel[...] += jnp.dot(block, hot, preferred_element_type=F32)
            return carry

        lax.fori_loop(0, 4, step, 0)
        return jnp.dot(weights_t[1, h], avg_sel[...].astype(BF), preferred_element_type=F32)

    self_sel[...] += dense(0)
    pass_on(1, 3)
    refreshed = self_sel[...] + dense(1)

    gain = jnp.concatenate([relation_b[...]] * 2, axis=1)
    queries = (refreshed.astype(BF).astype(F32) * gain).astype(BF)
    for copy in cand_x:
        copy.wait_recv()
    positive = jnp.zeros((1, 256), F32)
    for i in range(4):
        rows = jnp.concatenate([cand_all[i, 0], cand_all[i, 1]], axis=1).astype(F32)
        query = queries[i * W : (i + 1) * W].astype(F32)
        positive = positive + jnp.sum(query * rows, axis=0, keepdims=True)

    def softplus(v):
        return jnp.maximum(v, 0.0) + jnp.log1p(jnp.exp(-jnp.abs(v)))

    negative = jnp.dot(neg_rows[...], queries, preferred_element_type=F32)
    losses = softplus(-positive) + jnp.sum(softplus(negative), axis=0, keepdims=True) / 1024.0
    loss_ref[x, 0:1, :] = losses[:, 0:128]
    loss_ref[x, 1:2, :] = losses[:, 128:256]
    loss_copies = [
        remote(loss_ref.at[x], loss_ref.at[x], loss_ssem.at[dx], loss_rsem.at[dx], device(dx=dx))
        for dx in (1, 3, 2)
    ]
    for copy in loss_copies:
        copy.start()

    for da in (1, 3, 2):
        row_list(da).wait_send()
    for way in (1, 3):
        paper_copy(way).wait_send()
        paper_forward(way).wait_send()
        author_copy(way).wait_send()
        author_forward(way).wait_send()
    for copy in neg_x + cand_x:
        copy.wait_send()
    for db in (1, 3, 2):
        neg_copy(db).wait_send()
    for k in (0, 1, 2, 3, 4, 5, 7):
        cand_copy(k).wait_send()

    def main_drain(k, carry):
        @pl.when(k != 6)
        def _():
            for h in range(2):
                for da in range(4):
                    main_copy(da, k, h).wait_send()

        return carry

    lax.fori_loop(0, 8, main_drain, 0)

    def avg_drain(g, carry):
        for h in range(2):
            for dx in (1, 3):
                avg_copy(h, g, dx).wait_send()
                avg_forward(h, g, dx).wait_send()
        return carry

    lax.fori_loop(0, 4, avg_drain, 0)
    for copy in loss_copies:
        copy.wait()


def per_device(
    paper_feat,
    author_feat,
    weights,
    relation,
    send_rows,
    tile_src,
    tile_col,
    cand_author,
    cand_send,
    neg_rows,
):
    core = lax.axis_index("owner") % 2
    x = lax.axis_index("rep")

    def by_a(lists):
        lists = lists[0].reshape(4, 4, 2, -1)
        return jnp.where(core == 1, lists.transpose(1, 0, 2, 3), lists)

    rows = by_a(send_rows).reshape(4, 8, CAP)
    cands = by_a(cand_send).reshape(4, 1, 256)
    negs = jnp.broadcast_to(jnp.tile(neg_rows, (1, 4))[None], (4, 1, 128))
    last = jnp.concatenate([cands, negs, jnp.zeros((4, 1, 128), I32)], axis=2)
    idx = jnp.concatenate([rows, last, jnp.zeros((4, 7, CAP), I32)], axis=1)
    grid = cand_author.reshape(4, 4, 2, 32)
    first = lax.dynamic_index_in_dim(grid[:, :, 0], x, 1, keepdims=False).reshape(1, 128)
    second = lax.dynamic_index_in_dim(grid[:, :, 1], x, 0, keepdims=False).reshape(1, 128)
    edges = jnp.concatenate([first, second], axis=1)

    vmem = pl.BlockSpec(memory_space=pltpu.VMEM)
    dma = pltpu.SemaphoreType.DMA
    out, loss = pl.pallas_call(
        kernel,
        out_shape=(
            jax.ShapeDtypeStruct((W, ROWS), BF),
            jax.ShapeDtypeStruct((4, 8, 128), F32),
        ),
        in_specs=[
            pl.BlockSpec(memory_space=pltpu.SMEM),
            vmem,
            vmem,
            pl.BlockSpec(memory_space=pl.ANY),
            vmem,
            vmem,
            vmem,
            vmem,
        ],
        out_specs=(vmem, vmem),
        scratch_shapes=[
            pltpu.VMEM((4, W, ROWS), BF),
            pltpu.VMEM((4, W, ROWS), BF),
            pltpu.VMEM((4, 16, CAP), I32),
            pltpu.VMEM((4, 8, 2, 4, HALF, 128), BF),
            pltpu.VMEM((128, HALF, 128), BF),
            pltpu.VMEM((128, HALF, 128), BF),
            pltpu.VMEM((8, W, 128), F32),
            pltpu.VMEM((W, 128), F32),
            pltpu.VMEM((8, W, 128), BF),
            pltpu.VMEM((W, 128), BF),
            pltpu.VMEM((4, 2, W, 128), BF),
            pltpu.VMEM((4, 2, W, 128), BF),
            pltpu.VMEM((2, 4, 4, W, 128), BF),
            pltpu.VMEM((1024, D), BF),
            pltpu.VMEM((2, D, D), BF),
            pltpu.VMEM((2, 2, D, D // 2), BF),
            pltpu.VMEM((D, 128), F32),
            pltpu.VMEM((2, 4, 4, HALF, 512), BF),
            pltpu.VMEM((W, ROWS), F32),
            pltpu.VMEM((D, 256), F32),
            pltpu.VMEM((D // 2, 256), F32),
            pltpu.VMEM((ROWS, 256), BF),
            dma,
            dma((4,)),
            dma((4,)),
            dma((4,)),
            dma((4,)),
            dma((4,)),
            dma((4,)),
            dma((4,)),
            dma((4,)),
            dma((4,)),
            dma((4,)),
            dma((2, 4, 8)),
            dma((2, 32)),
            dma((8,)),
            dma((8,)),
            dma((4,)),
            dma((4,)),
            dma((4,)),
            dma((4,)),
            dma,
            dma,
            dma((4,)),
            dma((4,)),
            dma((2, 4, 4)),
            dma((2, 4, 4)),
            dma((2, 4, 4)),
            dma((2, 4, 4)),
            dma((4,)),
            dma((4,)),
        ],
        compiler_params=pltpu.CompilerParams(
            collective_id=0, has_side_effects=True, vmem_limit_bytes=60 * 2**20
        ),
        name="conv_and_score",
    )(
        tile_src[0],
        paper_feat,
        author_feat,
        weights,
        relation.reshape(6, 128),
        idx,
        tile_col[0],
        edges,
    )
    refreshed = out.T
    even = loss[:, 0].reshape(4, 4, 32).transpose(1, 0, 2)
    odd = loss[:, 1].reshape(4, 4, 32)
    return refreshed, jnp.stack([even, odd], axis=2).reshape(-1)


def solution(mesh):
    placed = (
        P("owner", "rep"),
        P("owner", "rep"),
        P(),
        P(),
        P("owner", None, None),
        P(None, None, "owner"),
        P(None, None, "owner"),
        P("owner"),
        P("owner", None, None),
        P("owner", None),
    )
    return jax.shard_map(
        per_device,
        mesh=mesh,
        in_specs=placed,
        out_specs=(P("owner", "rep"), P("owner")),
        check_vma=False,
    )
```

```python
import jax
import jax.numpy as jnp
from jax import lax
from jax.experimental import pallas as pl
from jax.experimental.pallas import tpu as pltpu
from jax.sharding import PartitionSpec as P

MESH = pl.DeviceIdType.MESH
BF = jnp.bfloat16
F32 = jnp.float32
I32 = jnp.int32

W = 192
ROWS = 2048
CAP = 512
HALF = 96
SLOTS = 48
D = 768


def iota(shape, dim):
    return lax.broadcasted_iota(I32, shape, dim)


def one_hot(rows, picks):
    return (iota((rows, picks.shape[1]), 0) == picks).astype(BF)


def kernel(
    src_ref,
    paper_ref,
    author_ref,
    weights_ref,
    col_hbm,
    relation_ref,
    rows_ref,
    cand_ref,
    neg_ref,
    edge_ref,
    out_ref,
    loss_out,
    col_ref,
    idx_ref,
    tiled,
    loss_ref,
    paper_t,
    author_t,
    idx_all,
    send_buf,
    recv_first,
    recv_second,
    cand_acc,
    neg_acc,
    cand_send,
    neg_send,
    cand_rx,
    cand_all,
    neg_all,
    neg_rows,
    weights_v,
    weights_t,
    relation_b,
    avg_all,
    self_part,
    self_sel,
    avg_sel,
    edge_hot,
    w_sem,
    in_sem,
    p1_send,
    p1_recv,
    f1_send,
    f1_recv,
    i1_send,
    i1_recv,
    au_send,
    au_recv,
    fa_send,
    fa_recv,
    main_send,
    main_recv,
    cand_ssem,
    cand_rsem,
    neg_ssem,
    neg_rsem,
    nx_send,
    nx_recv,
    swap_send,
    swap_recv,
    cx_send,
    cx_recv,
    avg_ssem,
    avg_rsem,
    fw_ssem,
    fw_rsem,
    loss_ssem,
    loss_rsem,
):
    recv = (recv_first, recv_second)
    owner = lax.axis_index("owner")
    x = lax.axis_index("rep")
    core = owner % 2
    y = (owner // 2) % 4
    z = owner // 8
    even = 1 - core
    a = z * even + y * core
    b = y * even + z * core

    def owner_at(a_pos, b_pos, core_pos):
        return (a_pos * even + b_pos * core) * 8 + (b_pos * even + a_pos * core) * 2 + core_pos

    def device(da=0, db=0, dcore=0, dx=0):
        return {
            "owner": owner_at((a + da) % 4, (b + db) % 4, (core + dcore) % 2),
            "rep": (x + dx) % 4,
        }

    def remote(src, dst, ssem, rsem, target):
        return pltpu.make_async_remote_copy(
            src_ref=src,
            dst_ref=dst,
            send_sem=ssem,
            recv_sem=rsem,
            device_id=target,
            device_id_type=MESH,
        )

    paper_in = pltpu.make_async_copy(paper_ref, paper_t.at[0], in_sem.at[0])
    author_in = pltpu.make_async_copy(author_ref, author_t.at[x], in_sem.at[1])
    col_in = pltpu.make_async_copy(col_hbm, col_ref, in_sem.at[2])
    weights_copy = pltpu.make_async_copy(weights_ref, weights_v, w_sem)
    paper_in.start()
    author_in.start()
    weights_copy.start()
    col_in.start()

    barrier = pltpu.get_barrier_semaphore()
    partners = [device(da=k) for k in (1, 2, 3)] + [device(db=k) for k in (1, 2, 3)]
    partners += [device(da=k, dcore=1) for k in (0, 1, 2, 3)]
    partners += [device(db=k, dcore=1) for k in (1, 2, 3)]
    partners += [device(dx=k) for k in (1, 2, 3)]
    for partner in partners:
        pl.semaphore_signal(barrier, inc=1, device_id=partner, device_id_type=MESH)

    lane_group = iota((1, 128), 1) // 32
    place = (iota((32, 128), 1) % 32 == iota((32, 128), 0)).astype(BF)

    def repeat_lanes(values):
        high = (values // 64).astype(F32).astype(BF)
        low = (values % 64).astype(F32).astype(BF)
        high = jnp.dot(high, place, preferred_element_type=F32)
        low = jnp.dot(low, place, preferred_element_type=F32)
        return (high * 64.0 + low).astype(I32)

    tiled[...] = repeat_lanes(cand_ref[...])
    neg_row = repeat_lanes(jnp.broadcast_to(neg_ref[...], (8, 32)))[0:1]
    for ap in range(4):
        for d in range(8):
            row = owner_at(ap, d // 2, d % 2)
            idx_ref[ap, d : d + 1, :] = rows_ref[pl.ds(row, 1), :]
        for j in range(2):
            line = jnp.zeros((1, 128), I32)
            for i in range(4):
                row = tiled[pl.ds(owner_at(ap, 2 * j + i // 2, i % 2), 1), :]
                line = jnp.where(lane_group == i, row, line)
            idx_ref[ap, 8:9, j * 128 : (j + 1) * 128] = line
        idx_ref[ap, 8:9, 256:384] = neg_row
    idx_all[0] = idx_ref[a]

    paper_in.wait()
    pl.semaphore_wait(barrier, len(partners))

    def row_list(da):
        slot = 4 - da
        return remote(
            idx_ref.at[(a + da) % 4], idx_all.at[slot], i1_send.at[slot], i1_recv.at[slot], device(da=da)
        )

    def paper_copy(da):
        slot = 4 - da
        return remote(
            paper_t.at[0], paper_t.at[slot], p1_send.at[slot], p1_recv.at[slot], device(da=da)
        )

    def half_of(way):
        return pl.ds(0 if way == 1 else HALF, HALF)

    def paper_forward(da):
        slot = 4 - da
        return remote(
            paper_t.at[slot, half_of(da)],
            paper_t.at[2, half_of(da)],
            f1_send.at[slot],
            f1_recv.at[slot],
            device(da=da),
        )

    def author_copy(dx):
        return remote(author_t.at[x], author_t.at[x], au_send.at[dx], au_recv.at[dx], device(dx=dx))

    def author_forward(dx):
        part = author_t.at[(x + 4 - dx) % 4, half_of(dx)]
        return remote(part, part, fa_send.at[dx], fa_recv.at[dx], device(dx=dx))

    for da in (1, 3, 2):
        row_list(da).start()
    for da in (1, 3):
        paper_copy(da).start()
    author_in.wait()
    for dx in (1, 3):
        author_copy(dx).start()

    def main_copy(da, k, h):
        db = (k // 2 + 1) % 4
        dcore = k % 2
        source = owner_at((a + da) % 4, b, core)
        return remote(
            send_buf.at[da, k, h],
            recv[h].at[pl.ds(4 * source, 4)],
            main_send.at[h, da, k],
            main_recv.at[h, source],
            device(db=db, dcore=dcore),
        )

    def main_start(da, k, h):
        @pl.when(k == 6)
        def _():
            source = owner_at((a + da) % 4, b, core)
            pltpu.make_async_copy(
                send_buf.at[da, k, h], recv[h].at[pl.ds(4 * source, 4)], main_recv.at[h, source]
            ).start()

        @pl.when(k != 6)
        def _():
            main_copy(da, k, h).start()

    def select_main(da):
        def step(k, carry):
            row = ((b + k // 2 + 1) % 4) * 2 + (core + k) % 2
            picks = idx_all[da, pl.ds(row, 1), :]
            out = jnp.dot(paper_t[da], one_hot(ROWS, picks), preferred_element_type=F32).astype(BF)
            for h in range(2):
                for j in range(4):
                    send_buf[da, k, h, j] = out[h * HALF : (h + 1) * HALF, j * 128 : (j + 1) * 128]
            main_start(da, k, 0)
            return carry

        lax.fori_loop(0, 8, step, 0)

    group = iota((W, 128), 1) // 32

    def select_extra(da):
        a_src = (a + da) % 4
        picks = idx_all[da, 8:9, 0:384]
        out = jnp.dot(paper_t[da], one_hot(ROWS, picks), preferred_element_type=F32)
        here = group == a_src
        for d in range(8):
            part = out[:, (d // 4) * 128 : (d // 4 + 1) * 128]
            part = pltpu.roll(part, ((a_src + 4 - d % 4) % 4) * 32, 1)
            old = jnp.zeros((W, 128), F32) if da == 0 else cand_acc[d]
            cand_acc[d] = jnp.where(here, part, old)
        old = jnp.zeros((W, 128), F32) if da == 0 else neg_acc[...]
        neg_acc[...] = jnp.where(here, out[:, 256:384], old)

    def cand_copy(k):
        return remote(
            cand_send.at[((b + k // 2 + 1) % 4) * 2 + (core + k) % 2],
            cand_rx.at[b, core],
            cand_ssem.at[k],
            cand_rsem.at[b * 2 + core],
            device(db=(k // 2 + 1) % 4, dcore=k % 2),
        )

    def cand_local():
        return pltpu.make_async_copy(
            cand_send.at[b * 2 + core], cand_rx.at[b, core], cand_rsem.at[b * 2 + core]
        )

    def neg_copy(db):
        return remote(
            neg_send, neg_all.at[core, x, b], neg_ssem.at[db], neg_rsem.at[b], device(db=db)
        )

    def neg_local():
        return pltpu.make_async_copy(neg_send, neg_all.at[core, x, b], neg_rsem.at[b])

    select_main(0)
    select_extra(0)
    weights_copy.wait()
    for w in range(2):
        for h in range(2):
            rows = [weights_v[w, pl.ds(i * W + h * HALF, HALF), :] for i in range(4)]
            weights_t[w, h] = jnp.transpose(jnp.concatenate(rows, axis=0))
    for i in range(6):
        row = jnp.broadcast_to(relation_ref[i : i + 1, :], (128, 128))
        relation_b[pl.ds(i * 128, 128), :] = jnp.transpose(row)
    halves = [jnp.zeros((8, 128), I32) for _ in range(2)]
    for i in range(4):
        row = jnp.broadcast_to(edge_ref[pl.ds(i * 2 + x // 2, 1), :], (8, 128))
        row = pltpu.roll(row, ((i + 4 - (x % 2) * 2) % 4) * 32, 1)
        halves[0] = jnp.where(lane_group == i, row, halves[0])
        row = jnp.broadcast_to(edge_ref[pl.ds(x * 2 + i // 2, 1), :], (8, 128))
        row = pltpu.roll(row, ((i + 3 - (i % 2) * 2) % 4) * 32, 1)
        halves[1] = jnp.where(lane_group == i, row, halves[1])
    edge_hot[...] = one_hot(ROWS, jnp.concatenate(halves, axis=1)[0:1])
    col_in.wait()

    for da in (1, 3):
        paper_copy(da).wait_recv()
        paper_forward(da).start()
    row_list(3).wait_recv()
    select_main(1)
    select_extra(1)
    row_list(1).wait_recv()
    select_main(3)
    select_extra(3)
    for dx in (1, 3):
        author_copy(dx).wait_recv()
        author_forward(dx).start()
    row_list(2).wait_recv()
    for da in (1, 3):
        paper_forward(da).wait_recv()
    select_extra(2)
    for d in range(8):
        cand_send[d] = cand_acc[d].astype(BF)
    neg_send[...] = neg_acc[...].astype(BF)
    for db in (1, 3, 2):
        neg_copy(db).start()
    neg_local().start()
    for k in (0, 1, 2, 3, 4, 5, 7):
        cand_copy(k).start()
    cand_local().start()
    select_main(2)

    def second_half(k, carry):
        for da in (0, 1, 3, 2):
            main_start(da, k, 1)
        return carry

    lax.fori_loop(0, 8, second_half, 0)

    for slot in range(4):
        pltpu.make_async_copy(neg_send, neg_all.at[core, x, slot], neg_rsem.at[slot]).wait()
    neg_x = [
        remote(neg_all.at[core, x], neg_all.at[core, x], nx_send.at[dx], nx_recv.at[dx], device(dx=dx))
        for dx in (1, 3, 2)
    ]
    for copy in neg_x:
        copy.start()
    for slot in range(8):
        pltpu.make_async_copy(
            cand_send.at[0], cand_rx.at[slot // 2, slot % 2], cand_rsem.at[slot]
        ).wait()
    cand_x = [
        remote(
            cand_rx.at[(x + dx) % 4], cand_all.at[x], cx_send.at[dx], cx_recv.at[dx], device(dx=dx)
        )
        for dx in (1, 3, 2)
    ]
    for copy in cand_x:
        copy.start()
    cand_all[x] = cand_rx[x]

    def avg_copy(h, g, dx):
        part = avg_all.at[h, x, g]
        return remote(part, part, avg_ssem.at[h, g, dx], avg_rsem.at[h, g, dx], device(dx=dx))

    def avg_forward(h, g, dx):
        part = avg_all.at[h, (x + 4 - dx) % 4, g, pl.ds(0 if dx == 1 else HALF // 2, HALF // 2)]
        return remote(part, part, fw_ssem.at[h, g, dx], fw_rsem.at[h, g, dx], device(dx=dx))

    def pass_on(h, g):
        for dx in (1, 3):
            avg_copy(h, g, dx).wait_recv()
            avg_forward(h, g, dx).start()

    def aggregate(h):
        def recv_wait(s, carry):
            pltpu.make_async_copy(
                send_buf.at[0, 0, h], recv[h].at[pl.ds(4 * s, 4)], main_recv.at[h, s]
            ).wait()
            return carry

        lax.fori_loop(0, 32, recv_wait, 0)

        def step(block, carry):
            lanes = pl.ds(pl.multiple_of(block * 128, 128), 128)
            live = (col_ref[:, lanes] < 128).astype(F32)
            scale = 1.0 / jnp.maximum(jnp.sum(live, axis=0, keepdims=True), 1.0)
            total = jnp.zeros((HALF, 128), F32)
            for t in range(0, SLOTS, 8):
                left = [recv[h][src_ref[block, t + i]] for i in range(8)]
                right = [one_hot(128, col_ref[t + i : t + i + 1, lanes]) for i in range(8)]
                total = total + jnp.dot(
                    jnp.concatenate(left, axis=1),
                    jnp.concatenate(right, axis=0),
                    preferred_element_type=F32,
                )
            g = block // 4
            inner = pl.ds(pl.multiple_of((block % 4) * 128, 128), 128)
            avg_all[h, x, g, :, inner] = (total * scale).astype(BF)

            @pl.when(block % 4 == 3)
            def _():
                for dx in (1, 3):
                    avg_copy(h, g, dx).start()

            @pl.when(block % 4 == 3)
            def _():
                @pl.when(g >= 2)
                def _():
                    pass_on(h, g - 2)

            return carry

        lax.fori_loop(0, 16, step, 0)

    aggregate(0)

    own_rows = pl.ds(pl.multiple_of(x * W, 16), W)
    pass_on(0, 2)
    for dx in (1, 3):
        author_forward(dx).wait_recv()
    for g in range(4):
        lanes = pl.ds(g * 512, 512)
        total = jnp.zeros((W, 512), F32)
        for h in range(2):
            block = [author_t[i, pl.ds(h * HALF, HALF), lanes] for i in range(4)]
            total = total + jnp.dot(
                weights_t[0, h, own_rows, :],
                jnp.concatenate(block, axis=0),
                preferred_element_type=F32,
            )
        self_part[:, lanes] = total
    pass_on(0, 3)
    author_sel = [
        jnp.dot(author_t[i], edge_hot[...], preferred_element_type=F32).astype(BF) for i in range(4)
    ]
    total = jnp.zeros((D, 256), F32)
    for h in range(2):
        block = [author_sel[i][h * HALF : (h + 1) * HALF] for i in range(4)]
        total = total + jnp.dot(
            weights_t[0, h], jnp.concatenate(block, axis=0), preferred_element_type=F32
        )
    self_sel[...] = total
    for copy in neg_x:
        copy.wait_recv()
    swap = remote(neg_all.at[core], neg_all.at[core], swap_send, swap_recv, device(dcore=1))
    swap.start()
    swap.wait()
    for c in range(2):
        for i in range(4):
            block = jnp.concatenate([neg_all[c, j, i] for j in range(4)], axis=0)
            neg_rows[pl.ds((c * 4 + i) * 128, 128), :] = jnp.transpose(block)

    aggregate(1)
    pass_on(1, 2)

    def dense(h):
        avg_sel[...] = jnp.zeros_like(avg_sel)

        def step(g, carry):
            for dx in (1, 3):
                avg_forward(h, g, dx).wait_recv()
            lanes = pl.ds(pl.multiple_of(g * 512, 512), 512)
            block = jnp.concatenate([avg_all[h, i, g] for i in range(4)], axis=0)
            mixed = self_part[:, lanes] + jnp.dot(
                weights_t[1, h, own_rows, :], block, preferred_element_type=F32
            )
            if h == 0:
                self_part[:, lanes] = mixed
            else:
                out_ref[:, lanes] = mixed.astype(BF)
            hot = edge_hot[pl.ds(pl.multiple_of(g * 512, 512), 512), :]
            avg_sel[...] += jnp.dot(block, hot, preferred_element_type=F32)
            return carry

        lax.fori_loop(0, 4, step, 0)
        return jnp.dot(weights_t[1, h], avg_sel[...].astype(BF), preferred_element_type=F32)

    self_sel[...] += dense(0)
    pass_on(1, 3)
    refreshed = self_sel[...] + dense(1)

    gain = jnp.concatenate([relation_b[...]] * 2, axis=1)
    queries = (refreshed.astype(BF).astype(F32) * gain).astype(BF)
    for copy in cand_x:
        copy.wait_recv()
    positive = jnp.zeros((1, 256), F32)
    for i in range(4):
        rows = jnp.concatenate([cand_all[i, 0], cand_all[i, 1]], axis=1).astype(F32)
        query = queries[i * W : (i + 1) * W].astype(F32)
        positive = positive + jnp.sum(query * rows, axis=0, keepdims=True)

    def softplus(v):
        return jnp.maximum(v, 0.0) + jnp.log1p(jnp.exp(-jnp.abs(v)))

    negative = jnp.dot(neg_rows[...], queries, preferred_element_type=F32)
    losses = softplus(-positive) + jnp.sum(softplus(negative), axis=0, keepdims=True) / 1024.0
    loss_ref[x, 0:1, :] = losses[:, 0:128]
    loss_ref[x, 1:2, :] = losses[:, 128:256]
    loss_copies = [
        remote(loss_ref.at[x], loss_ref.at[x], loss_ssem.at[dx], loss_rsem.at[dx], device(dx=dx))
        for dx in (1, 3, 2)
    ]
    for copy in loss_copies:
        copy.start()

    for da in (1, 3, 2):
        row_list(da).wait_send()
    for way in (1, 3):
        paper_copy(way).wait_send()
        paper_forward(way).wait_send()
        author_copy(way).wait_send()
        author_forward(way).wait_send()
    for copy in neg_x + cand_x:
        copy.wait_send()
    for db in (1, 3, 2):
        neg_copy(db).wait_send()
    for k in (0, 1, 2, 3, 4, 5, 7):
        cand_copy(k).wait_send()

    def main_drain(k, carry):
        @pl.when(k != 6)
        def _():
            for h in range(2):
                for da in range(4):
                    main_copy(da, k, h).wait_send()

        return carry

    lax.fori_loop(0, 8, main_drain, 0)

    def avg_drain(g, carry):
        for h in range(2):
            for dx in (1, 3):
                avg_copy(h, g, dx).wait_send()
                avg_forward(h, g, dx).wait_send()
        return carry

    lax.fori_loop(0, 4, avg_drain, 0)
    for copy in loss_copies:
        copy.wait()
    for r in range(8):
        line = jnp.zeros((8, 128), F32)
        for i in range(4):
            low = r % 2 * 2 + i // 2
            line_x, at = (low, r // 2) if i % 2 == 0 else (r // 2, low)
            row = jnp.broadcast_to(loss_ref[line_x, i % 2 : i % 2 + 1, :], (8, 128))
            row = pltpu.roll(row, ((i + 4 - at) % 4) * 32, 1)
            line = jnp.where(lane_group == i, row, line)
        loss_out[r : r + 1, :] = line[0:1]


def per_device(
    paper_feat,
    author_feat,
    weights,
    relation,
    send_rows,
    tile_src,
    tile_col,
    cand_author,
    cand_send,
    neg_rows,
):
    vmem = pl.BlockSpec(memory_space=pltpu.VMEM)
    any_space = pl.BlockSpec(memory_space=pl.ANY)
    dma = pltpu.SemaphoreType.DMA
    out, loss = pl.pallas_call(
        kernel,
        out_shape=(
            jax.ShapeDtypeStruct((W, ROWS), BF),
            jax.ShapeDtypeStruct((8, 128), F32),
        ),
        in_specs=[
            pl.BlockSpec(memory_space=pltpu.SMEM),
            any_space,
            any_space,
            any_space,
            any_space,
            vmem,
            vmem,
            vmem,
            vmem,
            vmem,
        ],
        out_specs=(vmem, vmem),
        scratch_shapes=[
            pltpu.VMEM((SLOTS, ROWS), I32),
            pltpu.VMEM((4, 16, CAP), I32),
            pltpu.VMEM((32, 128), I32),
            pltpu.VMEM((4, 8, 128), F32),
            pltpu.VMEM((4, W, ROWS), BF),
            pltpu.VMEM((4, W, ROWS), BF),
            pltpu.VMEM((4, 16, CAP), I32),
            pltpu.VMEM((4, 8, 2, 4, HALF, 128), BF),
            pltpu.VMEM((128, HALF, 128), BF),
            pltpu.VMEM((128, HALF, 128), BF),
            pltpu.VMEM((8, W, 128), F32),
            pltpu.VMEM((W, 128), F32),
            pltpu.VMEM((8, W, 128), BF),
            pltpu.VMEM((W, 128), BF),
            pltpu.VMEM((4, 2, W, 128), BF),
            pltpu.VMEM((4, 2, W, 128), BF),
            pltpu.VMEM((2, 4, 4, W, 128), BF),
            pltpu.VMEM((1024, D), BF),
            pltpu.VMEM((2, D, D), BF),
            pltpu.VMEM((2, 2, D, D // 2), BF),
            pltpu.VMEM((D, 128), F32),
            pltpu.VMEM((2, 4, 4, HALF, 512), BF),
            pltpu.VMEM((W, ROWS), F32),
            pltpu.VMEM((D, 256), F32),
            pltpu.VMEM((D // 2, 256), F32),
            pltpu.VMEM((ROWS, 256), BF),
            dma,
            dma((3,)),
            dma((4,)),
            dma((4,)),
            dma((4,)),
            dma((4,)),
            dma((4,)),
            dma((4,)),
            dma((4,)),
            dma((4,)),
            dma((4,)),
            dma((4,)),
            dma((2, 4, 8)),
            dma((2, 32)),
            dma((8,)),
            dma((8,)),
            dma((4,)),
            dma((4,)),
            dma((4,)),
            dma((4,)),
            dma,
            dma,
            dma((4,)),
            dma((4,)),
            dma((2, 4, 4)),
            dma((2, 4, 4)),
            dma((2, 4, 4)),
            dma((2, 4, 4)),
            dma((4,)),
            dma((4,)),
        ],
        compiler_params=pltpu.CompilerParams(
            collective_id=0, has_side_effects=True, vmem_limit_bytes=60 * 2**20
        ),
        name="conv_and_score",
    )(
        tile_src[0].T,
        paper_feat.T,
        author_feat.T,
        weights,
        tile_col[0],
        relation.reshape(6, 128),
        send_rows[0],
        cand_send[0],
        neg_rows,
        cand_author.reshape(8, 128),
    )
    return out.T, loss.reshape(-1)


def solution(mesh):
    placed = (
        P("owner", "rep"),
        P("owner", "rep"),
        P(),
        P(),
        P("owner", None, None),
        P(None, None, "owner"),
        P(None, None, "owner"),
        P("owner"),
        P("owner", None, None),
        P("owner", None),
    )
    return jax.shard_map(
        per_device,
        mesh=mesh,
        in_specs=placed,
        out_specs=(P("owner", "rep"), P("owner")),
        check_vma=False,
    )
```

```python
import jax
import jax.numpy as jnp
from jax import lax
from jax.experimental import pallas as pl
from jax.experimental.pallas import tpu as pltpu
from jax.sharding import PartitionSpec as P

MESH = pl.DeviceIdType.MESH
BF = jnp.bfloat16
F32 = jnp.float32
I32 = jnp.int32

W = 192
ROWS = 2048
CAP = 512
HALF = 96
PARTS = (96, 96)
STARTS = (0, 96)
N_PARTS = len(PARTS)
CHUNKS = 4
PER = 16 // CHUNKS
LANES = 128 * PER
SWAP_AT = 8
SLOTS = 48
D = 768


def iota(shape, dim):
    return lax.broadcasted_iota(I32, shape, dim)


def one_hot(rows, picks):
    return (iota((rows, picks.shape[1]), 0) == picks).astype(BF)


def kernel(
    src_ref,
    paper_ref,
    author_ref,
    weights_ref,
    col_hbm,
    relation_ref,
    rows_ref,
    cand_ref,
    neg_ref,
    edge_ref,
    out_ref,
    loss_out,
    col_ref,
    idx_ref,
    tiled,
    loss_ref,
    paper_t,
    author_t,
    idx_all,
    *rest,
):
    (send_buf, recv, weights_t, avg_all, avg_sel), rest = (
        [rest[i * N_PARTS : (i + 1) * N_PARTS] for i in range(5)],
        rest[5 * N_PARTS :],
    )
    (
        cand_acc,
        neg_acc,
        cand_send,
        neg_send,
        cand_rx,
        cand_all,
        neg_all,
        neg_rows,
        weights_v,
        relation_b,
        self_part,
        self_sel,
        edge_hot,
        w_sem,
        in_sem,
        p1_send,
        p1_recv,
        f1_send,
        f1_recv,
        i1_send,
        i1_recv,
        au_send,
        au_recv,
        fa_send,
        fa_recv,
        main_send,
        main_recv,
        cand_ssem,
        cand_rsem,
        neg_ssem,
        neg_rsem,
        nx_send,
        nx_recv,
        swap_send,
        swap_recv,
        cx_send,
        cx_recv,
        avg_ssem,
        avg_rsem,
        fw_ssem,
        fw_rsem,
        loss_ssem,
        loss_rsem,
    ) = rest
    owner = lax.axis_index("owner")
    x = lax.axis_index("rep")
    core = owner % 2
    y = (owner // 2) % 4
    z = owner // 8
    even = 1 - core
    a = z * even + y * core
    b = y * even + z * core

    def owner_at(a_pos, b_pos, core_pos):
        return (a_pos * even + b_pos * core) * 8 + (b_pos * even + a_pos * core) * 2 + core_pos

    def device(da=0, db=0, dcore=0, dx=0):
        return {
            "owner": owner_at((a + da) % 4, (b + db) % 4, (core + dcore) % 2),
            "rep": (x + dx) % 4,
        }

    def remote(src, dst, ssem, rsem, target):
        return pltpu.make_async_remote_copy(
            src_ref=src,
            dst_ref=dst,
            send_sem=ssem,
            recv_sem=rsem,
            device_id=target,
            device_id_type=MESH,
        )

    paper_in = pltpu.make_async_copy(paper_ref, paper_t.at[0], in_sem.at[0])
    author_in = pltpu.make_async_copy(author_ref, author_t.at[x], in_sem.at[1])
    col_in = pltpu.make_async_copy(col_hbm, col_ref, in_sem.at[2])
    weights_copy = pltpu.make_async_copy(weights_ref, weights_v, w_sem)
    paper_in.start()
    author_in.start()
    weights_copy.start()
    col_in.start()

    barrier = pltpu.get_barrier_semaphore()
    partners = [device(da=k) for k in (1, 2, 3)] + [device(db=k) for k in (1, 2, 3)]
    partners += [device(da=k, dcore=1) for k in (0, 1, 2, 3)]
    partners += [device(db=k, dcore=1) for k in (1, 2, 3)]
    partners += [device(dx=k) for k in (1, 2, 3)]
    for partner in partners:
        pl.semaphore_signal(barrier, inc=1, device_id=partner, device_id_type=MESH)

    lane_group = iota((1, 128), 1) // 32
    place = (iota((32, 128), 1) % 32 == iota((32, 128), 0)).astype(BF)

    def repeat_lanes(values):
        high = (values // 64).astype(F32).astype(BF)
        low = (values % 64).astype(F32).astype(BF)
        high = jnp.dot(high, place, preferred_element_type=F32)
        low = jnp.dot(low, place, preferred_element_type=F32)
        return (high * 64.0 + low).astype(I32)

    tiled[...] = repeat_lanes(cand_ref[...])
    neg_row = repeat_lanes(jnp.broadcast_to(neg_ref[...], (8, 32)))[0:1]
    for ap in range(4):
        for d in range(8):
            row = owner_at(ap, d // 2, d % 2)
            idx_ref[ap, d : d + 1, :] = rows_ref[pl.ds(row, 1), :]
        for j in range(2):
            line = jnp.zeros((1, 128), I32)
            for i in range(4):
                row = tiled[pl.ds(owner_at(ap, 2 * j + i // 2, i % 2), 1), :]
                line = jnp.where(lane_group == i, row, line)
            idx_ref[ap, 8:9, j * 128 : (j + 1) * 128] = line
        idx_ref[ap, 8:9, 256:384] = neg_row
    idx_all[0] = idx_ref[a]

    paper_in.wait()
    pl.semaphore_wait(barrier, len(partners))

    def row_list(da):
        slot = 4 - da
        return remote(
            idx_ref.at[(a + da) % 4], idx_all.at[slot], i1_send.at[slot], i1_recv.at[slot], device(da=da)
        )

    def paper_copy(da):
        slot = 4 - da
        return remote(
            paper_t.at[0], paper_t.at[slot], p1_send.at[slot], p1_recv.at[slot], device(da=da)
        )

    def half_of(way):
        return pl.ds(0 if way == 1 else HALF, HALF)

    def paper_forward(da):
        slot = 4 - da
        return remote(
            paper_t.at[slot, half_of(da)],
            paper_t.at[2, half_of(da)],
            f1_send.at[slot],
            f1_recv.at[slot],
            device(da=da),
        )

    def author_copy(dx):
        return remote(author_t.at[x], author_t.at[x], au_send.at[dx], au_recv.at[dx], device(dx=dx))

    def author_forward(dx):
        part = author_t.at[(x + 4 - dx) % 4, half_of(dx)]
        return remote(part, part, fa_send.at[dx], fa_recv.at[dx], device(dx=dx))

    for da in (1, 3, 2):
        row_list(da).start()
    for da in (1, 3):
        paper_copy(da).start()
    author_in.wait()
    for dx in (1, 3):
        author_copy(dx).start()

    def place_of(k):
        own = k // 6
        j = k % 3
        return (1 - own) * (1 + 2 * j - 3 * (j // 2)), (1 - own) * (k // 3) + own * (k - 6)

    def main_copy(da, k, h):
        db, dcore = place_of(k)
        source = owner_at((a + da) % 4, b, core)
        return remote(
            send_buf[h].at[da, k],
            recv[h].at[pl.ds(4 * source, 4)],
            main_send.at[h, da, k],
            main_recv.at[h, source],
            device(db=db, dcore=dcore),
        )

    def main_start(da, k, h):
        @pl.when(k == 6)
        def _():
            source = owner_at((a + da) % 4, b, core)
            pltpu.make_async_copy(
                send_buf[h].at[da, k], recv[h].at[pl.ds(4 * source, 4)], main_recv.at[h, source]
            ).start()

        @pl.when(k != 6)
        def _():
            main_copy(da, k, h).start()

    def select_main(da):
        def step(k, carry):
            db, dcore = place_of(k)
            row = ((b + db) % 4) * 2 + (core + dcore) % 2
            picks = idx_all[da, pl.ds(row, 1), :]
            out = jnp.dot(paper_t[da], one_hot(ROWS, picks), preferred_element_type=F32).astype(BF)
            for h in range(N_PARTS):
                for j in range(4):
                    rows = out[STARTS[h] : STARTS[h] + PARTS[h], j * 128 : (j + 1) * 128]
                    send_buf[h][da, k, j] = rows
            main_start(da, k, 0)
            return carry

        lax.fori_loop(0, 8, step, 0)

    group = iota((W, 128), 1) // 32

    def select_extra(da):
        a_src = (a + da) % 4
        picks = idx_all[da, 8:9, 0:384]
        out = jnp.dot(paper_t[da], one_hot(ROWS, picks), preferred_element_type=F32)
        here = group == a_src
        for d in range(8):
            part = out[:, (d // 4) * 128 : (d // 4 + 1) * 128]
            part = pltpu.roll(part, ((a_src + 4 - d % 4) % 4) * 32, 1)
            old = jnp.zeros((W, 128), F32) if da == 0 else cand_acc[d]
            cand_acc[d] = jnp.where(here, part, old)
        old = jnp.zeros((W, 128), F32) if da == 0 else neg_acc[...]
        neg_acc[...] = jnp.where(here, out[:, 256:384], old)

    def cand_copy(k):
        db, dcore = place_of(k)
        return remote(
            cand_send.at[((b + db) % 4) * 2 + (core + dcore) % 2],
            cand_rx.at[b, core],
            cand_ssem.at[k],
            cand_rsem.at[b * 2 + core],
            device(db=db, dcore=dcore),
        )

    def cand_local():
        return pltpu.make_async_copy(
            cand_send.at[b * 2 + core], cand_rx.at[b, core], cand_rsem.at[b * 2 + core]
        )

    def neg_copy(db):
        return remote(
            neg_send, neg_all.at[core, x, b], neg_ssem.at[db], neg_rsem.at[b], device(db=db)
        )

    def neg_local():
        return pltpu.make_async_copy(neg_send, neg_all.at[core, x, b], neg_rsem.at[b])

    select_main(0)
    select_extra(0)
    weights_copy.wait()
    for w in range(2):
        for h in range(N_PARTS):
            rows = [weights_v[w, pl.ds(i * W + STARTS[h], PARTS[h]), :] for i in range(4)]
            weights_t[h][w] = jnp.transpose(jnp.concatenate(rows, axis=0))
    for i in range(6):
        row = jnp.broadcast_to(relation_ref[i : i + 1, :], (128, 128))
        relation_b[pl.ds(i * 128, 128), :] = jnp.transpose(row)
    halves = [jnp.zeros((8, 128), I32) for _ in range(2)]
    for i in range(4):
        row = jnp.broadcast_to(edge_ref[pl.ds(i * 2 + x // 2, 1), :], (8, 128))
        row = pltpu.roll(row, ((i + 4 - (x % 2) * 2) % 4) * 32, 1)
        halves[0] = jnp.where(lane_group == i, row, halves[0])
        row = jnp.broadcast_to(edge_ref[pl.ds(x * 2 + i // 2, 1), :], (8, 128))
        row = pltpu.roll(row, ((i + 3 - (i % 2) * 2) % 4) * 32, 1)
        halves[1] = jnp.where(lane_group == i, row, halves[1])
    edge_hot[...] = one_hot(ROWS, jnp.concatenate(halves, axis=1)[0:1])
    col_in.wait()

    for da in (1, 3):
        paper_copy(da).wait_recv()
        paper_forward(da).start()
    row_list(3).wait_recv()
    select_main(1)
    select_extra(1)
    row_list(1).wait_recv()
    select_extra(3)
    row_list(2).wait_recv()
    for da in (1, 3):
        paper_forward(da).wait_recv()
    select_extra(2)
    for d in range(8):
        cand_send[d] = cand_acc[d].astype(BF)
    neg_send[...] = neg_acc[...].astype(BF)
    for db in (1, 3, 2):
        neg_copy(db).start()
    neg_local().start()
    for k in (0, 1, 2, 3, 4, 5, 7):
        cand_copy(k).start()
    cand_local().start()
    for dx in (1, 3):
        author_copy(dx).wait_recv()
        author_forward(dx).start()
    select_main(3)

    for slot in range(4):
        pltpu.make_async_copy(neg_send, neg_all.at[core, x, slot], neg_rsem.at[slot]).wait()
    neg_x = [
        remote(neg_all.at[core, x], neg_all.at[core, x], nx_send.at[dx], nx_recv.at[dx], device(dx=dx))
        for dx in (1, 3, 2)
    ]
    for copy in neg_x:
        copy.start()
    for slot in range(8):
        pltpu.make_async_copy(
            cand_send.at[0], cand_rx.at[slot // 2, slot % 2], cand_rsem.at[slot]
        ).wait()
    cand_x = [
        remote(
            cand_rx.at[(x + dx) % 4], cand_all.at[x], cx_send.at[dx], cx_recv.at[dx], device(dx=dx)
        )
        for dx in (1, 3, 2)
    ]
    for copy in cand_x:
        copy.start()
    cand_all[x] = cand_rx[x]
    select_main(2)

    def later_part(h):
        def step(k, carry):
            for da in (0, 1, 3, 2):
                main_start(da, k, h)
            return carry

        lax.fori_loop(0, 8, step, 0)

    for h in range(1, N_PARTS):
        later_part(h)

    def avg_copy(h, g, dx):
        part = avg_all[h].at[x, g]
        return remote(part, part, avg_ssem.at[h, g, dx], avg_rsem.at[h, g, dx], device(dx=dx))

    def avg_forward(h, g, dx):
        size = PARTS[h] // 2
        part = avg_all[h].at[(x + 4 - dx) % 4, g, pl.ds(0 if dx == 1 else size, size)]
        return remote(part, part, fw_ssem.at[h, g, dx], fw_rsem.at[h, g, dx], device(dx=dx))

    def pass_on(h, g):
        for dx in (1, 3):
            avg_copy(h, g, dx).wait_recv()
            avg_forward(h, g, dx).start()

    def aggregate(h, between):
        def recv_wait(s, carry):
            pltpu.make_async_copy(
                send_buf[h].at[0, 0], recv[h].at[pl.ds(4 * s, 4)], main_recv.at[h, s]
            ).wait()
            return carry

        lax.fori_loop(0, 32, recv_wait, 0)

        def step(block, carry):
            lanes = pl.ds(pl.multiple_of(block * 128, 128), 128)
            live = (col_ref[:, lanes] < 128).astype(F32)
            scale = 1.0 / jnp.maximum(jnp.sum(live, axis=0, keepdims=True), 1.0)
            total = jnp.zeros((PARTS[h], 128), F32)
            for t in range(0, SLOTS, 8):
                left = [recv[h][src_ref[block, t + i]] for i in range(8)]
                right = [one_hot(128, col_ref[t + i : t + i + 1, lanes]) for i in range(8)]
                total = total + jnp.dot(
                    jnp.concatenate(left, axis=1),
                    jnp.concatenate(right, axis=0),
                    preferred_element_type=F32,
                )
            g = block // PER
            inner = pl.ds(pl.multiple_of((block % PER) * 128, 128), 128)
            avg_all[h][x, g, :, inner] = (total * scale).astype(BF)

            @pl.when(block % PER == PER - 1)
            def _():
                for dx in (1, 3):
                    avg_copy(h, g, dx).start()

            @pl.when(block % PER == PER - 1)
            def _():
                @pl.when(g >= 2)
                def _():
                    pass_on(h, g - 2)

            for at, call in between:
                pl.when(block == at)(call)
            return carry

        lax.fori_loop(0, 16, step, 0)

    aggregate(0, [])

    own_rows = pl.ds(pl.multiple_of(x * W, 16), W)
    pass_on(0, CHUNKS - 2)
    for dx in (1, 3):
        author_forward(dx).wait_recv()
    for g in range(4):
        lanes = pl.ds(g * 512, 512)
        total = jnp.zeros((W, 512), F32)
        for h in range(N_PARTS):
            block = [author_t[i, pl.ds(STARTS[h], PARTS[h]), lanes] for i in range(4)]
            total = total + jnp.dot(
                weights_t[h][0, own_rows, :],
                jnp.concatenate(block, axis=0),
                preferred_element_type=F32,
            )
        self_part[:, lanes] = total
    pass_on(0, CHUNKS - 1)
    author_sel = [
        jnp.dot(author_t[i], edge_hot[...], preferred_element_type=F32).astype(BF) for i in range(4)
    ]
    total = jnp.zeros((D, 256), F32)
    for h in range(N_PARTS):
        block = [author_sel[i][STARTS[h] : STARTS[h] + PARTS[h]] for i in range(4)]
        total = total + jnp.dot(
            weights_t[h][0], jnp.concatenate(block, axis=0), preferred_element_type=F32
        )
    self_sel[...] = total
    swap = remote(neg_all.at[core], neg_all.at[core], swap_send, swap_recv, device(dcore=1))

    def swap_cores():
        for copy in neg_x:
            copy.wait_recv()
        swap.start()

    def dense(h):
        avg_sel[h][...] = jnp.zeros_like(avg_sel[h])

        def step(g, carry):
            for dx in (1, 3):
                avg_forward(h, g, dx).wait_recv()
            lanes = pl.ds(pl.multiple_of(g * LANES, LANES), LANES)
            block = jnp.concatenate([avg_all[h][i, g] for i in range(4)], axis=0)
            mixed = self_part[:, lanes] + jnp.dot(
                weights_t[h][1, own_rows, :], block, preferred_element_type=F32
            )
            if h < N_PARTS - 1:
                self_part[:, lanes] = mixed
            else:
                out_ref[:, lanes] = mixed.astype(BF)
            hot = edge_hot[lanes, :]
            avg_sel[h][...] += jnp.dot(block, hot, preferred_element_type=F32)
            return carry

        lax.fori_loop(0, CHUNKS, step, 0)
        return jnp.dot(weights_t[h][1], avg_sel[h][...].astype(BF), preferred_element_type=F32)

    for h in range(1, N_PARTS):
        between = []
        if h > 1:
            between.append((3, lambda: pass_on(h - 1, CHUNKS - 2)))
            between.append((7, lambda: pass_on(h - 1, CHUNKS - 1)))
        if h == 1:
            between.append((SWAP_AT, swap_cores))
        aggregate(h, between)
    pass_on(N_PARTS - 1, CHUNKS - 2)
    swap.wait()
    for c in range(2):
        for i in range(4):
            block = jnp.concatenate([neg_all[c, j, i] for j in range(4)], axis=0)
            neg_rows[pl.ds((c * 4 + i) * 128, 128), :] = jnp.transpose(block)
    pass_on(N_PARTS - 1, CHUNKS - 1)
    for h in range(N_PARTS - 1):
        self_sel[...] += dense(h)
    refreshed = self_sel[...] + dense(N_PARTS - 1)

    gain = jnp.concatenate([relation_b[...]] * 2, axis=1)
    queries = (refreshed.astype(BF).astype(F32) * gain).astype(BF)
    for copy in cand_x:
        copy.wait_recv()
    positive = jnp.zeros((1, 256), F32)
    for i in range(4):
        rows = jnp.concatenate([cand_all[i, 0], cand_all[i, 1]], axis=1).astype(F32)
        query = queries[i * W : (i + 1) * W].astype(F32)
        positive = positive + jnp.sum(query * rows, axis=0, keepdims=True)

    def softplus(v):
        return jnp.maximum(v, 0.0) + jnp.log1p(jnp.exp(-jnp.abs(v)))

    negative = jnp.dot(neg_rows[...], queries, preferred_element_type=F32)
    losses = softplus(-positive) + jnp.sum(softplus(negative), axis=0, keepdims=True) / 1024.0
    loss_ref[x, 0:1, :] = losses[:, 0:128]
    loss_ref[x, 1:2, :] = losses[:, 128:256]
    loss_copies = [
        remote(loss_ref.at[x], loss_ref.at[x], loss_ssem.at[dx], loss_rsem.at[dx], device(dx=dx))
        for dx in (1, 3, 2)
    ]
    for copy in loss_copies:
        copy.start()

    for da in (1, 3, 2):
        row_list(da).wait_send()
    for way in (1, 3):
        paper_copy(way).wait_send()
        paper_forward(way).wait_send()
        author_copy(way).wait_send()
        author_forward(way).wait_send()
    for copy in neg_x + cand_x:
        copy.wait_send()
    for db in (1, 3, 2):
        neg_copy(db).wait_send()
    for k in (0, 1, 2, 3, 4, 5, 7):
        cand_copy(k).wait_send()

    def main_drain(k, carry):
        @pl.when(k != 6)
        def _():
            for h in range(N_PARTS):
                for da in range(4):
                    main_copy(da, k, h).wait_send()

        return carry

    lax.fori_loop(0, 8, main_drain, 0)

    def avg_drain(g, carry):
        for h in range(N_PARTS):
            for dx in (1, 3):
                avg_copy(h, g, dx).wait_send()
                avg_forward(h, g, dx).wait_send()
        return carry

    lax.fori_loop(0, CHUNKS, avg_drain, 0)
    for copy in loss_copies:
        copy.wait()
    for r in range(8):
        line = jnp.zeros((8, 128), F32)
        for i in range(4):
            low = r % 2 * 2 + i // 2
            line_x, at = (low, r // 2) if i % 2 == 0 else (r // 2, low)
            row = jnp.broadcast_to(loss_ref[line_x, i % 2 : i % 2 + 1, :], (8, 128))
            row = pltpu.roll(row, ((i + 4 - at) % 4) * 32, 1)
            line = jnp.where(lane_group == i, row, line)
        loss_out[r : r + 1, :] = line[0:1]


def per_device(
    paper_feat,
    author_feat,
    weights,
    relation,
    send_rows,
    tile_src,
    tile_col,
    cand_author,
    cand_send,
    neg_rows,
):
    vmem = pl.BlockSpec(memory_space=pltpu.VMEM)
    any_space = pl.BlockSpec(memory_space=pl.ANY)
    dma = pltpu.SemaphoreType.DMA
    out, loss = pl.pallas_call(
        kernel,
        out_shape=(
            jax.ShapeDtypeStruct((W, ROWS), BF),
            jax.ShapeDtypeStruct((8, 128), F32),
        ),
        in_specs=[
            pl.BlockSpec(memory_space=pltpu.SMEM),
            any_space,
            any_space,
            any_space,
            any_space,
            vmem,
            vmem,
            vmem,
            vmem,
            vmem,
        ],
        out_specs=(vmem, vmem),
        scratch_shapes=[
            pltpu.VMEM((SLOTS, ROWS), I32),
            pltpu.VMEM((4, 16, CAP), I32),
            pltpu.VMEM((32, 128), I32),
            pltpu.VMEM((4, 8, 128), F32),
            pltpu.VMEM((4, W, ROWS), BF),
            pltpu.VMEM((4, W, ROWS), BF),
            pltpu.VMEM((4, 16, CAP), I32),
            *[pltpu.VMEM((4, 8, 4, n, 128), BF) for n in PARTS],
            *[pltpu.VMEM((128, n, 128), BF) for n in PARTS],
            *[pltpu.VMEM((2, D, 4 * n), BF) for n in PARTS],
            *[pltpu.VMEM((4, CHUNKS, n, LANES), BF) for n in PARTS],
            *[pltpu.VMEM((4 * n, 256), F32) for n in PARTS],
            pltpu.VMEM((8, W, 128), F32),
            pltpu.VMEM((W, 128), F32),
            pltpu.VMEM((8, W, 128), BF),
            pltpu.VMEM((W, 128), BF),
            pltpu.VMEM((4, 2, W, 128), BF),
            pltpu.VMEM((4, 2, W, 128), BF),
            pltpu.VMEM((2, 4, 4, W, 128), BF),
            pltpu.VMEM((1024, D), BF),
            pltpu.VMEM((2, D, D), BF),
            pltpu.VMEM((D, 128), F32),
            pltpu.VMEM((W, ROWS), F32),
            pltpu.VMEM((D, 256), F32),
            pltpu.VMEM((ROWS, 256), BF),
            dma,
            dma((3,)),
            dma((4,)),
            dma((4,)),
            dma((4,)),
            dma((4,)),
            dma((4,)),
            dma((4,)),
            dma((4,)),
            dma((4,)),
            dma((4,)),
            dma((4,)),
            dma((N_PARTS, 4, 8)),
            dma((N_PARTS, 32)),
            dma((8,)),
            dma((8,)),
            dma((4,)),
            dma((4,)),
            dma((4,)),
            dma((4,)),
            dma,
            dma,
            dma((4,)),
            dma((4,)),
            dma((N_PARTS, CHUNKS, 4)),
            dma((N_PARTS, CHUNKS, 4)),
            dma((N_PARTS, CHUNKS, 4)),
            dma((N_PARTS, CHUNKS, 4)),
            dma((4,)),
            dma((4,)),
        ],
        compiler_params=pltpu.CompilerParams(
            collective_id=0, has_side_effects=True, vmem_limit_bytes=60 * 2**20
        ),
        name="conv_and_score",
    )(
        tile_src[0].T,
        paper_feat.T,
        author_feat.T,
        weights,
        tile_col[0],
        relation.reshape(6, 128),
        send_rows[0],
        cand_send[0],
        neg_rows,
        cand_author.reshape(8, 128),
    )
    return out.T, loss.reshape(-1)


def solution(mesh):
    placed = (
        P("owner", "rep"),
        P("owner", "rep"),
        P(),
        P(),
        P("owner", None, None),
        P(None, None, "owner"),
        P(None, None, "owner"),
        P("owner"),
        P("owner", None, None),
        P("owner", None),
    )
    return jax.shard_map(
        per_device,
        mesh=mesh,
        in_specs=placed,
        out_specs=(P("owner", "rep"), P("owner")),
        check_vma=False,
    )
```

```python
import jax
import jax.numpy as jnp
from jax import lax
from jax.experimental import pallas as pl
from jax.experimental.pallas import tpu as pltpu
from jax.sharding import PartitionSpec as P

MESH = pl.DeviceIdType.MESH
BF = jnp.bfloat16
F32 = jnp.float32
I32 = jnp.int32

W = 192
ROWS = 2048
CAP = 512
HALF = 96
PARTS = (96, 96)
STARTS = (0, 96)
N_PARTS = len(PARTS)
CHUNKS = 4
PER = 16 // CHUNKS
LANES = 128 * PER
SWAP_AT = 8
SLOTS = 48
D = 768


def iota(shape, dim):
    return lax.broadcasted_iota(I32, shape, dim)


def one_hot(rows, picks):
    return (iota((rows, picks.shape[1]), 0) == picks).astype(BF)


def kernel(
    src_ref,
    paper_ref,
    author_ref,
    weights_ref,
    col_hbm,
    relation_ref,
    rows_ref,
    cand_ref,
    neg_ref,
    edge_ref,
    out_ref,
    loss_out,
    col_ref,
    idx_ref,
    tiled,
    loss_ref,
    paper_t,
    author_t,
    idx_all,
    *rest,
):
    (send_buf, recv, weights_t, avg_all, avg_sel), rest = (
        [rest[i * N_PARTS : (i + 1) * N_PARTS] for i in range(5)],
        rest[5 * N_PARTS :],
    )
    (
        cand_acc,
        neg_acc,
        cand_send,
        neg_send,
        cand_rx,
        cand_all,
        neg_all,
        neg_rows,
        weights_v,
        relation_b,
        self_part,
        self_sel,
        edge_hot,
        w_sem,
        in_sem,
        p1_send,
        p1_recv,
        f1_send,
        f1_recv,
        i1_send,
        i1_recv,
        au_send,
        au_recv,
        fa_send,
        fa_recv,
        main_send,
        main_recv,
        cand_ssem,
        cand_rsem,
        neg_ssem,
        neg_rsem,
        nx_send,
        nx_recv,
        swap_send,
        swap_recv,
        cx_send,
        cx_recv,
        avg_ssem,
        avg_rsem,
        fw_ssem,
        fw_rsem,
        loss_ssem,
        loss_rsem,
    ) = rest
    owner = lax.axis_index("owner")
    x = lax.axis_index("rep")
    core = owner % 2
    y = (owner // 2) % 4
    z = owner // 8
    even = 1 - core
    a = z * even + y * core
    b = y * even + z * core

    def owner_at(a_pos, b_pos, core_pos):
        return (a_pos * even + b_pos * core) * 8 + (b_pos * even + a_pos * core) * 2 + core_pos

    def device(da=0, db=0, dcore=0, dx=0):
        return {
            "owner": owner_at((a + da) % 4, (b + db) % 4, (core + dcore) % 2),
            "rep": (x + dx) % 4,
        }

    def remote(src, dst, ssem, rsem, target):
        return pltpu.make_async_remote_copy(
            src_ref=src,
            dst_ref=dst,
            send_sem=ssem,
            recv_sem=rsem,
            device_id=target,
            device_id_type=MESH,
        )

    paper_in = pltpu.make_async_copy(paper_ref, paper_t.at[0], in_sem.at[0])
    author_in = pltpu.make_async_copy(author_ref, author_t.at[x], in_sem.at[1])
    col_in = pltpu.make_async_copy(col_hbm, col_ref, in_sem.at[2])
    weights_copy = pltpu.make_async_copy(weights_ref, weights_v, w_sem)
    paper_in.start()
    author_in.start()
    weights_copy.start()
    col_in.start()

    barrier = pltpu.get_barrier_semaphore()
    partners = [device(da=k) for k in (1, 2, 3)] + [device(db=k) for k in (1, 2, 3)]
    partners += [device(da=k, dcore=1) for k in (0, 1, 2, 3)]
    partners += [device(db=k, dcore=1) for k in (1, 2, 3)]
    partners += [device(dx=k) for k in (1, 2, 3)]
    for partner in partners:
        pl.semaphore_signal(barrier, inc=1, device_id=partner, device_id_type=MESH)

    lane_group = iota((1, 128), 1) // 32
    place = (iota((32, 128), 1) % 32 == iota((32, 128), 0)).astype(BF)

    def repeat_lanes(values):
        high = (values // 64).astype(F32).astype(BF)
        low = (values % 64).astype(F32).astype(BF)
        high = jnp.dot(high, place, preferred_element_type=F32)
        low = jnp.dot(low, place, preferred_element_type=F32)
        return (high * 64.0 + low).astype(I32)

    tiled[...] = repeat_lanes(cand_ref[...])
    neg_row = repeat_lanes(jnp.broadcast_to(neg_ref[...], (8, 32)))[0:1]
    for ap in range(4):
        for d in range(8):
            row = owner_at(ap, d // 2, d % 2)
            idx_ref[ap, d : d + 1, :] = rows_ref[pl.ds(row, 1), :]
        for j in range(2):
            line = jnp.zeros((1, 128), I32)
            for i in range(4):
                row = tiled[pl.ds(owner_at(ap, 2 * j + i // 2, i % 2), 1), :]
                line = jnp.where(lane_group == i, row, line)
            idx_ref[ap, 8:9, j * 128 : (j + 1) * 128] = line
        idx_ref[ap, 8:9, 256:384] = neg_row
    idx_all[0] = idx_ref[a]

    paper_in.wait()
    pl.semaphore_wait(barrier, len(partners))

    def row_list(da):
        slot = 4 - da
        return remote(
            idx_ref.at[(a + da) % 4], idx_all.at[slot], i1_send.at[slot], i1_recv.at[slot], device(da=da)
        )

    def paper_copy(da):
        slot = 4 - da
        return remote(
            paper_t.at[0], paper_t.at[slot], p1_send.at[slot], p1_recv.at[slot], device(da=da)
        )

    def half_of(way):
        return pl.ds(0 if way == 1 else HALF, HALF)

    def paper_forward(da):
        slot = 4 - da
        return remote(
            paper_t.at[slot, half_of(da)],
            paper_t.at[2, half_of(da)],
            f1_send.at[slot],
            f1_recv.at[slot],
            device(da=da),
        )

    def author_copy(dx):
        return remote(author_t.at[x], author_t.at[x], au_send.at[dx], au_recv.at[dx], device(dx=dx))

    def author_forward(dx):
        part = author_t.at[(x + 4 - dx) % 4, half_of(dx)]
        return remote(part, part, fa_send.at[dx], fa_recv.at[dx], device(dx=dx))

    for da in (1, 3, 2):
        row_list(da).start()
    for da in (1, 3):
        paper_copy(da).start()
    author_in.wait()
    for dx in (1, 3):
        author_copy(dx).start()

    def place_of(k):
        own = k // 6
        j = k % 3
        return (1 - own) * (1 + 2 * j - 3 * (j // 2)), (1 - own) * (k // 3) + own * (k - 6)

    def main_copy(da, k, h):
        db, dcore = place_of(k)
        source = owner_at((a + da) % 4, b, core)
        return remote(
            send_buf[h].at[da, k],
            recv[h].at[pl.ds(4 * source, 4)],
            main_send.at[h, da, k],
            main_recv.at[h, source],
            device(db=db, dcore=dcore),
        )

    def main_start(da, k, h):
        @pl.when(k == 6)
        def _():
            source = owner_at((a + da) % 4, b, core)
            pltpu.make_async_copy(
                send_buf[h].at[da, k], recv[h].at[pl.ds(4 * source, 4)], main_recv.at[h, source]
            ).start()

        @pl.when(k != 6)
        def _():
            main_copy(da, k, h).start()

    def select_main(da):
        def step(k, carry):
            db, dcore = place_of(k)
            row = ((b + db) % 4) * 2 + (core + dcore) % 2
            picks = idx_all[da, pl.ds(row, 1), :]
            out = jnp.dot(paper_t[da], one_hot(ROWS, picks), preferred_element_type=F32).astype(BF)
            for h in range(N_PARTS):
                for j in range(4):
                    rows = out[STARTS[h] : STARTS[h] + PARTS[h], j * 128 : (j + 1) * 128]
                    send_buf[h][da, k, j] = rows
            main_start(da, k, 0)
            return carry

        lax.fori_loop(0, 8, step, 0)

    group = iota((W, 128), 1) // 32

    def select_extra(da):
        a_src = (a + da) % 4
        picks = idx_all[da, 8:9, 0:384]
        out = jnp.dot(paper_t[da], one_hot(ROWS, picks), preferred_element_type=F32)
        here = group == a_src
        for d in range(8):
            part = out[:, (d // 4) * 128 : (d // 4 + 1) * 128]
            part = pltpu.roll(part, ((a_src + 4 - d % 4) % 4) * 32, 1)
            old = jnp.zeros((W, 128), F32) if da == 0 else cand_acc[d]
            cand_acc[d] = jnp.where(here, part, old)
        old = jnp.zeros((W, 128), F32) if da == 0 else neg_acc[...]
        neg_acc[...] = jnp.where(here, out[:, 256:384], old)

    def cand_copy(k):
        db, dcore = place_of(k)
        return remote(
            cand_send.at[((b + db) % 4) * 2 + (core + dcore) % 2],
            cand_rx.at[b, core],
            cand_ssem.at[k],
            cand_rsem.at[b * 2 + core],
            device(db=db, dcore=dcore),
        )

    def cand_local():
        return pltpu.make_async_copy(
            cand_send.at[b * 2 + core], cand_rx.at[b, core], cand_rsem.at[b * 2 + core]
        )

    def neg_copy(db):
        return remote(
            neg_send, neg_all.at[core, x, b], neg_ssem.at[db], neg_rsem.at[b], device(db=db)
        )

    def neg_local():
        return pltpu.make_async_copy(neg_send, neg_all.at[core, x, b], neg_rsem.at[b])

    select_main(0)
    select_extra(0)
    weights_copy.wait()
    for w in range(2):
        for h in range(N_PARTS):
            rows = [weights_v[w, pl.ds(i * W + STARTS[h], PARTS[h]), :] for i in range(4)]
            weights_t[h][w] = jnp.transpose(jnp.concatenate(rows, axis=0))
    for i in range(6):
        row = jnp.broadcast_to(relation_ref[i : i + 1, :], (128, 128))
        relation_b[pl.ds(i * 128, 128), :] = jnp.transpose(row)
    halves = [jnp.zeros((8, 128), I32) for _ in range(2)]
    for i in range(4):
        row = jnp.broadcast_to(edge_ref[pl.ds(i * 2 + x // 2, 1), :], (8, 128))
        row = pltpu.roll(row, ((i + 4 - (x % 2) * 2) % 4) * 32, 1)
        halves[0] = jnp.where(lane_group == i, row, halves[0])
        row = jnp.broadcast_to(edge_ref[pl.ds(x * 2 + i // 2, 1), :], (8, 128))
        row = pltpu.roll(row, ((i + 3 - (i % 2) * 2) % 4) * 32, 1)
        halves[1] = jnp.where(lane_group == i, row, halves[1])
    edge_hot[...] = one_hot(ROWS, jnp.concatenate(halves, axis=1)[0:1])
    col_in.wait()

    for da in (1, 3):
        paper_copy(da).wait_recv()
        paper_forward(da).start()
    row_list(3).wait_recv()
    select_main(1)
    select_extra(1)
    row_list(1).wait_recv()
    select_extra(3)
    row_list(2).wait_recv()
    for da in (1, 3):
        paper_forward(da).wait_recv()
    select_extra(2)
    for d in range(8):
        cand_send[d] = cand_acc[d].astype(BF)
    neg_send[...] = neg_acc[...].astype(BF)
    for db in (1, 3, 2):
        neg_copy(db).start()
    neg_local().start()
    for k in (0, 1, 2, 3, 4, 5, 7):
        cand_copy(k).start()
    cand_local().start()
    for dx in (1, 3):
        author_copy(dx).wait_recv()
        author_forward(dx).start()
    select_main(3)

    for slot in range(4):
        pltpu.make_async_copy(neg_send, neg_all.at[core, x, slot], neg_rsem.at[slot]).wait()
    neg_x = [
        remote(neg_all.at[core, x], neg_all.at[core, x], nx_send.at[dx], nx_recv.at[dx], device(dx=dx))
        for dx in (1, 3, 2)
    ]
    for copy in neg_x:
        copy.start()
    for slot in range(8):
        pltpu.make_async_copy(
            cand_send.at[0], cand_rx.at[slot // 2, slot % 2], cand_rsem.at[slot]
        ).wait()
    cand_x = [
        remote(
            cand_rx.at[(x + dx) % 4], cand_all.at[x], cx_send.at[dx], cx_recv.at[dx], device(dx=dx)
        )
        for dx in (1, 3, 2)
    ]
    for copy in cand_x:
        copy.start()
    cand_all[x] = cand_rx[x]
    select_main(2)

    def later_part(h):
        def step(k, carry):
            for da in (0, 1, 3, 2):
                main_start(da, k, h)
            return carry

        lax.fori_loop(0, 8, step, 0)

    for h in range(1, N_PARTS):
        later_part(h)

    def avg_copy(h, g, dx):
        part = avg_all[h].at[x, g]
        return remote(part, part, avg_ssem.at[h, g, dx], avg_rsem.at[h, g, dx], device(dx=dx))

    def avg_forward(h, g, dx):
        size = PARTS[h] // 2
        part = avg_all[h].at[(x + 4 - dx) % 4, g, pl.ds(0 if dx == 1 else size, size)]
        return remote(part, part, fw_ssem.at[h, g, dx], fw_rsem.at[h, g, dx], device(dx=dx))

    def pass_on(h, g):
        for dx in (1, 3):
            avg_copy(h, g, dx).wait_recv()
            avg_forward(h, g, dx).start()

    def aggregate(h, between):
        def recv_wait(s, carry):
            pltpu.make_async_copy(
                send_buf[h].at[0, 0], recv[h].at[pl.ds(4 * s, 4)], main_recv.at[h, s]
            ).wait()
            return carry

        lax.fori_loop(0, 32, recv_wait, 0)

        def step(block, carry):
            lanes = pl.ds(pl.multiple_of(block * 128, 128), 128)
            live = (col_ref[:, lanes] < 128).astype(F32)
            scale = 1.0 / jnp.maximum(jnp.sum(live, axis=0, keepdims=True), 1.0)
            total = jnp.zeros((PARTS[h], 128), F32)
            for t in range(0, SLOTS, 8):
                left = [recv[h][src_ref[block, t + i]] for i in range(8)]
                right = [one_hot(128, col_ref[t + i : t + i + 1, lanes]) for i in range(8)]
                total = total + jnp.dot(
                    jnp.concatenate(left, axis=1),
                    jnp.concatenate(right, axis=0),
                    preferred_element_type=F32,
                )
            g = block // PER
            inner = pl.ds(pl.multiple_of((block % PER) * 128, 128), 128)
            avg_all[h][x, g, :, inner] = (total * scale).astype(BF)

            @pl.when(block % PER == PER - 1)
            def _():
                for dx in (1, 3):
                    avg_copy(h, g, dx).start()

            @pl.when(block % PER == PER - 1)
            def _():
                @pl.when(g >= 3)
                def _():
                    pass_on(h, g - 3)

            for at, call in between:
                pl.when(block == at)(call)
            return carry

        lax.fori_loop(0, 16, step, 0)

    aggregate(0, [])

    own_rows = pl.ds(pl.multiple_of(x * W, 16), W)
    pass_on(0, CHUNKS - 3)
    pass_on(0, CHUNKS - 2)
    for dx in (1, 3):
        author_forward(dx).wait_recv()
    for g in range(4):
        lanes = pl.ds(g * 512, 512)
        total = jnp.zeros((W, 512), F32)
        for h in range(N_PARTS):
            block = [author_t[i, pl.ds(STARTS[h], PARTS[h]), lanes] for i in range(4)]
            total = total + jnp.dot(
                weights_t[h][0, own_rows, :],
                jnp.concatenate(block, axis=0),
                preferred_element_type=F32,
            )
        self_part[:, lanes] = total
    pass_on(0, CHUNKS - 1)
    author_sel = [
        jnp.dot(author_t[i], edge_hot[...], preferred_element_type=F32).astype(BF) for i in range(4)
    ]
    total = jnp.zeros((D, 256), F32)
    for h in range(N_PARTS):
        block = [author_sel[i][STARTS[h] : STARTS[h] + PARTS[h]] for i in range(4)]
        total = total + jnp.dot(
            weights_t[h][0], jnp.concatenate(block, axis=0), preferred_element_type=F32
        )
    self_sel[...] = total
    swap = remote(neg_all.at[core], neg_all.at[core], swap_send, swap_recv, device(dcore=1))

    def swap_cores():
        for copy in neg_x:
            copy.wait_recv()
        swap.start()

    def dense(h):
        avg_sel[h][...] = jnp.zeros_like(avg_sel[h])

        def step(g, carry):
            for dx in (1, 3):
                avg_forward(h, g, dx).wait_recv()
            lanes = pl.ds(pl.multiple_of(g * LANES, LANES), LANES)
            block = jnp.concatenate([avg_all[h][i, g] for i in range(4)], axis=0)
            mixed = self_part[:, lanes] + jnp.dot(
                weights_t[h][1, own_rows, :], block, preferred_element_type=F32
            )
            if h < N_PARTS - 1:
                self_part[:, lanes] = mixed
            else:
                out_ref[:, lanes] = mixed.astype(BF)
            hot = edge_hot[lanes, :]
            avg_sel[h][...] += jnp.dot(block, hot, preferred_element_type=F32)
            return carry

        lax.fori_loop(0, CHUNKS, step, 0)
        return jnp.dot(weights_t[h][1], avg_sel[h][...].astype(BF), preferred_element_type=F32)

    for h in range(1, N_PARTS):
        between = []
        if h > 1:
            between.append((3, lambda: pass_on(h - 1, CHUNKS - 2)))
            between.append((7, lambda: pass_on(h - 1, CHUNKS - 1)))
        if h == 1:
            between.append((SWAP_AT, swap_cores))
        aggregate(h, between)
    pass_on(N_PARTS - 1, CHUNKS - 3)
    pass_on(N_PARTS - 1, CHUNKS - 2)
    swap.wait()
    for c in range(2):
        for i in range(4):
            block = jnp.concatenate([neg_all[c, j, i] for j in range(4)], axis=0)
            neg_rows[pl.ds((c * 4 + i) * 128, 128), :] = jnp.transpose(block)
    pass_on(N_PARTS - 1, CHUNKS - 1)
    for h in range(N_PARTS - 1):
        self_sel[...] += dense(h)
    refreshed = self_sel[...] + dense(N_PARTS - 1)

    gain = jnp.concatenate([relation_b[...]] * 2, axis=1)
    queries = (refreshed.astype(BF).astype(F32) * gain).astype(BF)
    for copy in cand_x:
        copy.wait_recv()
    positive = jnp.zeros((1, 256), F32)
    for i in range(4):
        rows = jnp.concatenate([cand_all[i, 0], cand_all[i, 1]], axis=1).astype(F32)
        query = queries[i * W : (i + 1) * W].astype(F32)
        positive = positive + jnp.sum(query * rows, axis=0, keepdims=True)

    def softplus(v):
        return jnp.maximum(v, 0.0) + jnp.log1p(jnp.exp(-jnp.abs(v)))

    negative = jnp.dot(neg_rows[...], queries, preferred_element_type=F32)
    losses = softplus(-positive) + jnp.sum(softplus(negative), axis=0, keepdims=True) / 1024.0
    loss_ref[x, 0:1, :] = losses[:, 0:128]
    loss_ref[x, 1:2, :] = losses[:, 128:256]
    loss_copies = [
        remote(loss_ref.at[x], loss_ref.at[x], loss_ssem.at[dx], loss_rsem.at[dx], device(dx=dx))
        for dx in (1, 3, 2)
    ]
    for copy in loss_copies:
        copy.start()

    for da in (1, 3, 2):
        row_list(da).wait_send()
    for way in (1, 3):
        paper_copy(way).wait_send()
        paper_forward(way).wait_send()
        author_copy(way).wait_send()
        author_forward(way).wait_send()
    for copy in neg_x + cand_x:
        copy.wait_send()
    for db in (1, 3, 2):
        neg_copy(db).wait_send()
    for k in (0, 1, 2, 3, 4, 5, 7):
        cand_copy(k).wait_send()

    def main_drain(k, carry):
        @pl.when(k != 6)
        def _():
            for h in range(N_PARTS):
                for da in range(4):
                    main_copy(da, k, h).wait_send()

        return carry

    lax.fori_loop(0, 8, main_drain, 0)

    def avg_drain(g, carry):
        for h in range(N_PARTS):
            for dx in (1, 3):
                avg_copy(h, g, dx).wait_send()
                avg_forward(h, g, dx).wait_send()
        return carry

    lax.fori_loop(0, CHUNKS, avg_drain, 0)
    for copy in loss_copies:
        copy.wait()
    for r in range(8):
        line = jnp.zeros((8, 128), F32)
        for i in range(4):
            low = r % 2 * 2 + i // 2
            line_x, at = (low, r // 2) if i % 2 == 0 else (r // 2, low)
            row = jnp.broadcast_to(loss_ref[line_x, i % 2 : i % 2 + 1, :], (8, 128))
            row = pltpu.roll(row, ((i + 4 - at) % 4) * 32, 1)
            line = jnp.where(lane_group == i, row, line)
        loss_out[r : r + 1, :] = line[0:1]


def per_device(
    paper_feat,
    author_feat,
    weights,
    relation,
    send_rows,
    tile_src,
    tile_col,
    cand_author,
    cand_send,
    neg_rows,
):
    vmem = pl.BlockSpec(memory_space=pltpu.VMEM)
    any_space = pl.BlockSpec(memory_space=pl.ANY)
    dma = pltpu.SemaphoreType.DMA
    out, loss = pl.pallas_call(
        kernel,
        out_shape=(
            jax.ShapeDtypeStruct((W, ROWS), BF),
            jax.ShapeDtypeStruct((8, 128), F32),
        ),
        in_specs=[
            pl.BlockSpec(memory_space=pltpu.SMEM),
            any_space,
            any_space,
            any_space,
            any_space,
            vmem,
            vmem,
            vmem,
            vmem,
            vmem,
        ],
        out_specs=(vmem, vmem),
        scratch_shapes=[
            pltpu.VMEM((SLOTS, ROWS), I32),
            pltpu.VMEM((4, 16, CAP), I32),
            pltpu.VMEM((32, 128), I32),
            pltpu.VMEM((4, 8, 128), F32),
            pltpu.VMEM((4, W, ROWS), BF),
            pltpu.VMEM((4, W, ROWS), BF),
            pltpu.VMEM((4, 16, CAP), I32),
            *[pltpu.VMEM((4, 8, 4, n, 128), BF) for n in PARTS],
            *[pltpu.VMEM((128, n, 128), BF) for n in PARTS],
            *[pltpu.VMEM((2, D, 4 * n), BF) for n in PARTS],
            *[pltpu.VMEM((4, CHUNKS, n, LANES), BF) for n in PARTS],
            *[pltpu.VMEM((4 * n, 256), F32) for n in PARTS],
            pltpu.VMEM((8, W, 128), F32),
            pltpu.VMEM((W, 128), F32),
            pltpu.VMEM((8, W, 128), BF),
            pltpu.VMEM((W, 128), BF),
            pltpu.VMEM((4, 2, W, 128), BF),
            pltpu.VMEM((4, 2, W, 128), BF),
            pltpu.VMEM((2, 4, 4, W, 128), BF),
            pltpu.VMEM((1024, D), BF),
            pltpu.VMEM((2, D, D), BF),
            pltpu.VMEM((D, 128), F32),
            pltpu.VMEM((W, ROWS), F32),
            pltpu.VMEM((D, 256), F32),
            pltpu.VMEM((ROWS, 256), BF),
            dma,
            dma((3,)),
            dma((4,)),
            dma((4,)),
            dma((4,)),
            dma((4,)),
            dma((4,)),
            dma((4,)),
            dma((4,)),
            dma((4,)),
            dma((4,)),
            dma((4,)),
            dma((N_PARTS, 4, 8)),
            dma((N_PARTS, 32)),
            dma((8,)),
            dma((8,)),
            dma((4,)),
            dma((4,)),
            dma((4,)),
            dma((4,)),
            dma,
            dma,
            dma((4,)),
            dma((4,)),
            dma((N_PARTS, CHUNKS, 4)),
            dma((N_PARTS, CHUNKS, 4)),
            dma((N_PARTS, CHUNKS, 4)),
            dma((N_PARTS, CHUNKS, 4)),
            dma((4,)),
            dma((4,)),
        ],
        compiler_params=pltpu.CompilerParams(
            collective_id=0, has_side_effects=True, vmem_limit_bytes=60 * 2**20
        ),
        name="conv_and_score",
    )(
        tile_src[0].T,
        paper_feat.T,
        author_feat.T,
        weights,
        tile_col[0],
        relation.reshape(6, 128),
        send_rows[0],
        cand_send[0],
        neg_rows,
        cand_author.reshape(8, 128),
    )
    def hand_over(out_in, loss_in, out_to, loss_to):
        out_to[...] = out_in[...]
        loss_to[...] = loss_in[...]

    out, loss = pl.pallas_call(
        hand_over,
        out_shape=(
            jax.ShapeDtypeStruct((W, ROWS), BF),
            jax.ShapeDtypeStruct((8, 128), F32),
        ),
        in_specs=[vmem, vmem],
        out_specs=(vmem, vmem),
        name="hand_over",
    )(out, loss)
    return out.T, loss.reshape(-1)


def solution(mesh):
    placed = (
        P("owner", "rep"),
        P("owner", "rep"),
        P(),
        P(),
        P("owner", None, None),
        P(None, None, "owner"),
        P(None, None, "owner"),
        P("owner"),
        P("owner", None, None),
        P("owner", None),
    )
    return jax.shard_map(
        per_device,
        mesh=mesh,
        in_specs=placed,
        out_specs=(P("owner", "rep"), P("owner")),
        check_vma=False,
    )
```

```python
import jax
import jax.numpy as jnp
from jax import lax
from jax.experimental import pallas as pl
from jax.experimental.pallas import tpu as pltpu
from jax.sharding import PartitionSpec as P

MESH = pl.DeviceIdType.MESH
BF = jnp.bfloat16
F32 = jnp.float32
I32 = jnp.int32

W = 192
ROWS = 2048
CAP = 512
HALF = 96
PARTS = (96, 96)
STARTS = (0, 96)
N_PARTS = len(PARTS)
CHUNKS = 4
PER = 16 // CHUNKS
LANES = 128 * PER
SWAP_AT = 8
SLOTS = 48
D = 768


def iota(shape, dim):
    return lax.broadcasted_iota(I32, shape, dim)


def one_hot(rows, picks):
    return (iota((rows, picks.shape[1]), 0) == picks).astype(BF)


def kernel(
    src_ref,
    paper_ref,
    author_ref,
    weights_ref,
    col_hbm,
    relation_ref,
    rows_ref,
    cand_ref,
    neg_ref,
    edge_ref,
    out_ref,
    loss_out,
    col_ref,
    idx_ref,
    tiled,
    loss_ref,
    paper_t,
    author_t,
    idx_all,
    *rest,
):
    (send_buf, recv, weights_t, avg_all, avg_sel), rest = (
        [rest[i * N_PARTS : (i + 1) * N_PARTS] for i in range(5)],
        rest[5 * N_PARTS :],
    )
    (
        cand_acc,
        neg_acc,
        cand_send,
        neg_send,
        cand_rx,
        cand_all,
        neg_all,
        neg_rows,
        weights_v,
        relation_b,
        self_part,
        self_sel,
        edge_hot,
        w_sem,
        in_sem,
        p1_send,
        p1_recv,
        f1_send,
        f1_recv,
        i1_send,
        i1_recv,
        au_send,
        au_recv,
        fa_send,
        fa_recv,
        main_send,
        main_recv,
        cand_ssem,
        cand_rsem,
        neg_ssem,
        neg_rsem,
        nx_send,
        nx_recv,
        swap_send,
        swap_recv,
        cx_send,
        cx_recv,
        avg_ssem,
        avg_rsem,
        fw_ssem,
        fw_rsem,
        loss_ssem,
        loss_rsem,
    ) = rest
    owner = lax.axis_index("owner")
    x = lax.axis_index("rep")
    core = owner % 2
    y = (owner // 2) % 4
    z = owner // 8
    even = 1 - core
    a = z * even + y * core
    b = y * even + z * core

    def owner_at(a_pos, b_pos, core_pos):
        return (a_pos * even + b_pos * core) * 8 + (b_pos * even + a_pos * core) * 2 + core_pos

    def device(da=0, db=0, dcore=0, dx=0):
        return {
            "owner": owner_at((a + da) % 4, (b + db) % 4, (core + dcore) % 2),
            "rep": (x + dx) % 4,
        }

    def remote(src, dst, ssem, rsem, target):
        return pltpu.make_async_remote_copy(
            src_ref=src,
            dst_ref=dst,
            send_sem=ssem,
            recv_sem=rsem,
            device_id=target,
            device_id_type=MESH,
        )

    paper_in = pltpu.make_async_copy(paper_ref, paper_t.at[0], in_sem.at[0])
    author_in = pltpu.make_async_copy(author_ref, author_t.at[x], in_sem.at[1])
    col_in = pltpu.make_async_copy(col_hbm, col_ref, in_sem.at[2])
    weights_copy = pltpu.make_async_copy(weights_ref, weights_v, w_sem)
    paper_in.start()
    author_in.start()
    weights_copy.start()
    col_in.start()

    barrier = pltpu.get_barrier_semaphore()
    partners = [device(da=k) for k in (1, 2, 3)] + [device(db=k) for k in (1, 2, 3)]
    partners += [device(da=k, dcore=1) for k in (0, 1, 2, 3)]
    partners += [device(db=k, dcore=1) for k in (1, 2, 3)]
    partners += [device(dx=k) for k in (1, 2, 3)]
    for partner in partners:
        pl.semaphore_signal(barrier, inc=1, device_id=partner, device_id_type=MESH)

    lane_group = iota((1, 128), 1) // 32
    place = (iota((32, 128), 1) % 32 == iota((32, 128), 0)).astype(BF)

    def repeat_lanes(values):
        high = (values // 64).astype(F32).astype(BF)
        low = (values % 64).astype(F32).astype(BF)
        high = jnp.dot(high, place, preferred_element_type=F32)
        low = jnp.dot(low, place, preferred_element_type=F32)
        return (high * 64.0 + low).astype(I32)

    tiled[...] = repeat_lanes(cand_ref[...])
    neg_row = repeat_lanes(jnp.broadcast_to(neg_ref[...], (8, 32)))[0:1]
    for ap in range(4):
        for d in range(8):
            row = owner_at(ap, d // 2, d % 2)
            idx_ref[ap, d : d + 1, :] = rows_ref[pl.ds(row, 1), :]
        for j in range(2):
            line = jnp.zeros((1, 128), I32)
            for i in range(4):
                row = tiled[pl.ds(owner_at(ap, 2 * j + i // 2, i % 2), 1), :]
                line = jnp.where(lane_group == i, row, line)
            idx_ref[ap, 8:9, j * 128 : (j + 1) * 128] = line
        idx_ref[ap, 8:9, 256:384] = neg_row
    idx_all[0] = idx_ref[a]

    paper_in.wait()
    pl.semaphore_wait(barrier, len(partners))

    def row_list(da):
        slot = 4 - da
        return remote(
            idx_ref.at[(a + da) % 4], idx_all.at[slot], i1_send.at[slot], i1_recv.at[slot], device(da=da)
        )

    def paper_copy(da):
        slot = 4 - da
        return remote(
            paper_t.at[0], paper_t.at[slot], p1_send.at[slot], p1_recv.at[slot], device(da=da)
        )

    def half_of(way):
        return pl.ds(0 if way == 1 else HALF, HALF)

    def paper_forward(da):
        slot = 4 - da
        return remote(
            paper_t.at[slot, half_of(da)],
            paper_t.at[2, half_of(da)],
            f1_send.at[slot],
            f1_recv.at[slot],
            device(da=da),
        )

    def author_copy(dx):
        return remote(author_t.at[x], author_t.at[x], au_send.at[dx], au_recv.at[dx], device(dx=dx))

    def author_forward(dx):
        part = author_t.at[(x + 4 - dx) % 4, half_of(dx)]
        return remote(part, part, fa_send.at[dx], fa_recv.at[dx], device(dx=dx))

    for da in (1, 3, 2):
        row_list(da).start()
    for da in (1, 3):
        paper_copy(da).start()
    author_in.wait()
    for dx in (1, 3):
        author_copy(dx).start()

    def place_of(k):
        own = k // 6
        j = k % 3
        return (1 - own) * (1 + 2 * j - 3 * (j // 2)), (1 - own) * (k // 3) + own * (k - 6)

    def main_copy(da, k, h):
        db, dcore = place_of(k)
        source = owner_at((a + da) % 4, b, core)
        return remote(
            send_buf[h].at[da, k],
            recv[h].at[pl.ds(4 * source, 4)],
            main_send.at[h, da, k],
            main_recv.at[h, source],
            device(db=db, dcore=dcore),
        )

    def main_start(da, k, h):
        @pl.when(k == 6)
        def _():
            source = owner_at((a + da) % 4, b, core)
            pltpu.make_async_copy(
                send_buf[h].at[da, k], recv[h].at[pl.ds(4 * source, 4)], main_recv.at[h, source]
            ).start()

        @pl.when(k != 6)
        def _():
            main_copy(da, k, h).start()

    def select_main(da):
        def step(k, carry):
            db, dcore = place_of(k)
            row = ((b + db) % 4) * 2 + (core + dcore) % 2
            picks = idx_all[da, pl.ds(row, 1), :]
            out = jnp.dot(paper_t[da], one_hot(ROWS, picks), preferred_element_type=F32).astype(BF)
            for h in range(N_PARTS):
                for j in range(4):
                    rows = out[STARTS[h] : STARTS[h] + PARTS[h], j * 128 : (j + 1) * 128]
                    send_buf[h][da, k, j] = rows
            main_start(da, k, 0)
            return carry

        lax.fori_loop(0, 8, step, 0)

    group = iota((W, 128), 1) // 32

    def select_extra(da):
        a_src = (a + da) % 4
        picks = idx_all[da, 8:9, 0:384]
        out = jnp.dot(paper_t[da], one_hot(ROWS, picks), preferred_element_type=F32)
        here = group == a_src
        for d in range(8):
            part = out[:, (d // 4) * 128 : (d // 4 + 1) * 128]
            part = pltpu.roll(part, ((a_src + 4 - d % 4) % 4) * 32, 1)
            old = jnp.zeros((W, 128), F32) if da == 0 else cand_acc[d]
            cand_acc[d] = jnp.where(here, part, old)
        old = jnp.zeros((W, 128), F32) if da == 0 else neg_acc[...]
        neg_acc[...] = jnp.where(here, out[:, 256:384], old)

    def cand_copy(k):
        db, dcore = place_of(k)
        return remote(
            cand_send.at[((b + db) % 4) * 2 + (core + dcore) % 2],
            cand_rx.at[b, core],
            cand_ssem.at[k],
            cand_rsem.at[b * 2 + core],
            device(db=db, dcore=dcore),
        )

    def cand_local():
        return pltpu.make_async_copy(
            cand_send.at[b * 2 + core], cand_rx.at[b, core], cand_rsem.at[b * 2 + core]
        )

    def neg_copy(db):
        return remote(
            neg_send, neg_all.at[core, x, b], neg_ssem.at[db], neg_rsem.at[b], device(db=db)
        )

    def neg_local():
        return pltpu.make_async_copy(neg_send, neg_all.at[core, x, b], neg_rsem.at[b])

    select_main(0)
    select_extra(0)
    weights_copy.wait()
    for w in range(2):
        for h in range(N_PARTS):
            rows = [weights_v[w, pl.ds(i * W + STARTS[h], PARTS[h]), :] for i in range(4)]
            weights_t[h][w] = jnp.transpose(jnp.concatenate(rows, axis=0))
    for i in range(6):
        row = jnp.broadcast_to(relation_ref[i : i + 1, :], (128, 128))
        relation_b[pl.ds(i * 128, 128), :] = jnp.transpose(row)
    halves = [jnp.zeros((8, 128), I32) for _ in range(2)]
    for i in range(4):
        row = jnp.broadcast_to(edge_ref[pl.ds(i * 2 + x // 2, 1), :], (8, 128))
        row = pltpu.roll(row, ((i + 4 - (x % 2) * 2) % 4) * 32, 1)
        halves[0] = jnp.where(lane_group == i, row, halves[0])
        row = jnp.broadcast_to(edge_ref[pl.ds(x * 2 + i // 2, 1), :], (8, 128))
        row = pltpu.roll(row, ((i + 3 - (i % 2) * 2) % 4) * 32, 1)
        halves[1] = jnp.where(lane_group == i, row, halves[1])
    edge_hot[...] = one_hot(ROWS, jnp.concatenate(halves, axis=1)[0:1])
    col_in.wait()

    for da in (1, 3):
        paper_copy(da).wait_recv()
        paper_forward(da).start()
    row_list(3).wait_recv()
    select_main(1)
    for dx in (1, 3):
        author_copy(dx).wait_recv()
        author_forward(dx).start()
    select_extra(1)
    row_list(1).wait_recv()
    select_extra(3)
    row_list(2).wait_recv()
    for da in (1, 3):
        paper_forward(da).wait_recv()
    select_extra(2)
    for d in range(8):
        cand_send[d] = cand_acc[d].astype(BF)
    neg_send[...] = neg_acc[...].astype(BF)
    for db in (1, 3, 2):
        neg_copy(db).start()
    neg_local().start()
    for k in (0, 1, 2, 3, 4, 5, 7):
        cand_copy(k).start()
    cand_local().start()
    select_main(3)

    for slot in range(4):
        pltpu.make_async_copy(neg_send, neg_all.at[core, x, slot], neg_rsem.at[slot]).wait()
    neg_x = [
        remote(neg_all.at[core, x], neg_all.at[core, x], nx_send.at[dx], nx_recv.at[dx], device(dx=dx))
        for dx in (1, 3, 2)
    ]
    for copy in neg_x:
        copy.start()
    for slot in range(8):
        pltpu.make_async_copy(
            cand_send.at[0], cand_rx.at[slot // 2, slot % 2], cand_rsem.at[slot]
        ).wait()
    cand_x = [
        remote(
            cand_rx.at[(x + dx) % 4], cand_all.at[x], cx_send.at[dx], cx_recv.at[dx], device(dx=dx)
        )
        for dx in (1, 3, 2)
    ]
    for copy in cand_x:
        copy.start()
    cand_all[x] = cand_rx[x]
    select_main(2)

    def later_part(h):
        def step(k, carry):
            for da in (0, 1, 3, 2):
                main_start(da, k, h)
            return carry

        lax.fori_loop(0, 8, step, 0)

    for h in range(1, N_PARTS):
        later_part(h)

    def avg_copy(h, g, dx):
        part = avg_all[h].at[x, g]
        return remote(part, part, avg_ssem.at[h, g, dx], avg_rsem.at[h, g, dx], device(dx=dx))

    def avg_forward(h, g, dx):
        size = PARTS[h] // 2
        part = avg_all[h].at[(x + 4 - dx) % 4, g, pl.ds(0 if dx == 1 else size, size)]
        return remote(part, part, fw_ssem.at[h, g, dx], fw_rsem.at[h, g, dx], device(dx=dx))

    def pass_on(h, g):
        for dx in (1, 3):
            avg_copy(h, g, dx).wait_recv()
            avg_forward(h, g, dx).start()

    def aggregate(h, between):
        def recv_wait(s, carry):
            pltpu.make_async_copy(
                send_buf[h].at[0, 0], recv[h].at[pl.ds(4 * s, 4)], main_recv.at[h, s]
            ).wait()
            return carry

        lax.fori_loop(0, 32, recv_wait, 0)

        def step(block, carry):
            lanes = pl.ds(pl.multiple_of(block * 128, 128), 128)
            live = (col_ref[:, lanes] < 128).astype(F32)
            scale = 1.0 / jnp.maximum(jnp.sum(live, axis=0, keepdims=True), 1.0)
            total = jnp.zeros((PARTS[h], 128), F32)
            for t in range(0, SLOTS, 8):
                left = [recv[h][src_ref[block, t + i]] for i in range(8)]
                right = [one_hot(128, col_ref[t + i : t + i + 1, lanes]) for i in range(8)]
                total = total + jnp.dot(
                    jnp.concatenate(left, axis=1),
                    jnp.concatenate(right, axis=0),
                    preferred_element_type=F32,
                )
            g = block // PER
            inner = pl.ds(pl.multiple_of((block % PER) * 128, 128), 128)
            avg_all[h][x, g, :, inner] = (total * scale).astype(BF)

            @pl.when(block % PER == PER - 1)
            def _():
                for dx in (1, 3):
                    avg_copy(h, g, dx).start()

            @pl.when(block % PER == PER - 1)
            def _():
                @pl.when(g >= 3)
                def _():
                    pass_on(h, g - 3)

            for at, call in between:
                pl.when(block == at)(call)
            return carry

        lax.fori_loop(0, 16, step, 0)

    aggregate(0, [])

    own_rows = pl.ds(pl.multiple_of(x * W, 16), W)
    pass_on(0, CHUNKS - 3)
    pass_on(0, CHUNKS - 2)
    for dx in (1, 3):
        author_forward(dx).wait_recv()
    for g in range(4):
        lanes = pl.ds(g * 512, 512)
        total = jnp.zeros((W, 512), F32)
        for h in range(N_PARTS):
            block = [author_t[i, pl.ds(STARTS[h], PARTS[h]), lanes] for i in range(4)]
            total = total + jnp.dot(
                weights_t[h][0, own_rows, :],
                jnp.concatenate(block, axis=0),
                preferred_element_type=F32,
            )
        self_part[:, lanes] = total
    pass_on(0, CHUNKS - 1)
    author_sel = [
        jnp.dot(author_t[i], edge_hot[...], preferred_element_type=F32).astype(BF) for i in range(4)
    ]
    total = jnp.zeros((D, 256), F32)
    for h in range(N_PARTS):
        block = [author_sel[i][STARTS[h] : STARTS[h] + PARTS[h]] for i in range(4)]
        total = total + jnp.dot(
            weights_t[h][0], jnp.concatenate(block, axis=0), preferred_element_type=F32
        )
    self_sel[...] = total
    swap = remote(neg_all.at[core], neg_all.at[core], swap_send, swap_recv, device(dcore=1))

    def swap_cores():
        for copy in neg_x:
            copy.wait_recv()
        swap.start()

    def dense(h):
        avg_sel[h][...] = jnp.zeros_like(avg_sel[h])

        def step(g, carry):
            for dx in (1, 3):
                avg_forward(h, g, dx).wait_recv()
            lanes = pl.ds(pl.multiple_of(g * LANES, LANES), LANES)
            block = jnp.concatenate([avg_all[h][i, g] for i in range(4)], axis=0)
            mixed = self_part[:, lanes] + jnp.dot(
                weights_t[h][1, own_rows, :], block, preferred_element_type=F32
            )
            if h < N_PARTS - 1:
                self_part[:, lanes] = mixed
            else:
                out_ref[:, lanes] = mixed.astype(BF)
            hot = edge_hot[lanes, :]
            avg_sel[h][...] += jnp.dot(block, hot, preferred_element_type=F32)
            return carry

        lax.fori_loop(0, CHUNKS, step, 0)
        return jnp.dot(weights_t[h][1], avg_sel[h][...].astype(BF), preferred_element_type=F32)

    for h in range(1, N_PARTS):
        between = []
        if h > 1:
            between.append((3, lambda: pass_on(h - 1, CHUNKS - 2)))
            between.append((7, lambda: pass_on(h - 1, CHUNKS - 1)))
        if h == 1:
            between.append((SWAP_AT, swap_cores))
        aggregate(h, between)
    pass_on(N_PARTS - 1, CHUNKS - 3)
    pass_on(N_PARTS - 1, CHUNKS - 2)
    swap.wait()
    for c in range(2):
        for i in range(4):
            block = jnp.concatenate([neg_all[c, j, i] for j in range(4)], axis=0)
            neg_rows[pl.ds((c * 4 + i) * 128, 128), :] = jnp.transpose(block)
    pass_on(N_PARTS - 1, CHUNKS - 1)
    for h in range(N_PARTS - 1):
        self_sel[...] += dense(h)
    refreshed = self_sel[...] + dense(N_PARTS - 1)

    gain = jnp.concatenate([relation_b[...]] * 2, axis=1)
    queries = (refreshed.astype(BF).astype(F32) * gain).astype(BF)
    for copy in cand_x:
        copy.wait_recv()
    positive = jnp.zeros((1, 256), F32)
    for i in range(4):
        rows = jnp.concatenate([cand_all[i, 0], cand_all[i, 1]], axis=1).astype(F32)
        query = queries[i * W : (i + 1) * W].astype(F32)
        positive = positive + jnp.sum(query * rows, axis=0, keepdims=True)

    def softplus(v):
        return jnp.maximum(v, 0.0) + jnp.log1p(jnp.exp(-jnp.abs(v)))

    negative = jnp.dot(neg_rows[...], queries, preferred_element_type=F32)
    losses = softplus(-positive) + jnp.sum(softplus(negative), axis=0, keepdims=True) / 1024.0
    loss_ref[x, 0:1, :] = losses[:, 0:128]
    loss_ref[x, 1:2, :] = losses[:, 128:256]
    loss_copies = [
        remote(loss_ref.at[x], loss_ref.at[x], loss_ssem.at[dx], loss_rsem.at[dx], device(dx=dx))
        for dx in (1, 3, 2)
    ]
    for copy in loss_copies:
        copy.start()

    for da in (1, 3, 2):
        row_list(da).wait_send()
    for way in (1, 3):
        paper_copy(way).wait_send()
        paper_forward(way).wait_send()
        author_copy(way).wait_send()
        author_forward(way).wait_send()
    for copy in neg_x + cand_x:
        copy.wait_send()
    for db in (1, 3, 2):
        neg_copy(db).wait_send()
    for k in (0, 1, 2, 3, 4, 5, 7):
        cand_copy(k).wait_send()

    def main_drain(k, carry):
        @pl.when(k != 6)
        def _():
            for h in range(N_PARTS):
                for da in range(4):
                    main_copy(da, k, h).wait_send()

        return carry

    lax.fori_loop(0, 8, main_drain, 0)

    def avg_drain(g, carry):
        for h in range(N_PARTS):
            for dx in (1, 3):
                avg_copy(h, g, dx).wait_send()
                avg_forward(h, g, dx).wait_send()
        return carry

    lax.fori_loop(0, CHUNKS, avg_drain, 0)
    for copy in loss_copies:
        copy.wait()
    for r in range(8):
        line = jnp.zeros((8, 128), F32)
        for i in range(4):
            low = r % 2 * 2 + i // 2
            line_x, at = (low, r // 2) if i % 2 == 0 else (r // 2, low)
            row = jnp.broadcast_to(loss_ref[line_x, i % 2 : i % 2 + 1, :], (8, 128))
            row = pltpu.roll(row, ((i + 4 - at) % 4) * 32, 1)
            line = jnp.where(lane_group == i, row, line)
        loss_out[r : r + 1, :] = line[0:1]


def per_device(
    paper_feat,
    author_feat,
    weights,
    relation,
    send_rows,
    tile_src,
    tile_col,
    cand_author,
    cand_send,
    neg_rows,
):
    vmem = pl.BlockSpec(memory_space=pltpu.VMEM)
    any_space = pl.BlockSpec(memory_space=pl.ANY)
    dma = pltpu.SemaphoreType.DMA
    out, loss = pl.pallas_call(
        kernel,
        out_shape=(
            jax.ShapeDtypeStruct((W, ROWS), BF),
            jax.ShapeDtypeStruct((8, 128), F32),
        ),
        in_specs=[
            pl.BlockSpec(memory_space=pltpu.SMEM),
            any_space,
            any_space,
            any_space,
            any_space,
            vmem,
            vmem,
            vmem,
            vmem,
            vmem,
        ],
        out_specs=(vmem, vmem),
        scratch_shapes=[
            pltpu.VMEM((SLOTS, ROWS), I32),
            pltpu.VMEM((4, 16, CAP), I32),
            pltpu.VMEM((32, 128), I32),
            pltpu.VMEM((4, 8, 128), F32),
            pltpu.VMEM((4, W, ROWS), BF),
            pltpu.VMEM((4, W, ROWS), BF),
            pltpu.VMEM((4, 16, CAP), I32),
            *[pltpu.VMEM((4, 8, 4, n, 128), BF) for n in PARTS],
            *[pltpu.VMEM((128, n, 128), BF) for n in PARTS],
            *[pltpu.VMEM((2, D, 4 * n), BF) for n in PARTS],
            *[pltpu.VMEM((4, CHUNKS, n, LANES), BF) for n in PARTS],
            *[pltpu.VMEM((4 * n, 256), F32) for n in PARTS],
            pltpu.VMEM((8, W, 128), F32),
            pltpu.VMEM((W, 128), F32),
            pltpu.VMEM((8, W, 128), BF),
            pltpu.VMEM((W, 128), BF),
            pltpu.VMEM((4, 2, W, 128), BF),
            pltpu.VMEM((4, 2, W, 128), BF),
            pltpu.VMEM((2, 4, 4, W, 128), BF),
            pltpu.VMEM((1024, D), BF),
            pltpu.VMEM((2, D, D), BF),
            pltpu.VMEM((D, 128), F32),
            pltpu.VMEM((W, ROWS), F32),
            pltpu.VMEM((D, 256), F32),
            pltpu.VMEM((ROWS, 256), BF),
            dma,
            dma((3,)),
            dma((4,)),
            dma((4,)),
            dma((4,)),
            dma((4,)),
            dma((4,)),
            dma((4,)),
            dma((4,)),
            dma((4,)),
            dma((4,)),
            dma((4,)),
            dma((N_PARTS, 4, 8)),
            dma((N_PARTS, 32)),
            dma((8,)),
            dma((8,)),
            dma((4,)),
            dma((4,)),
            dma((4,)),
            dma((4,)),
            dma,
            dma,
            dma((4,)),
            dma((4,)),
            dma((N_PARTS, CHUNKS, 4)),
            dma((N_PARTS, CHUNKS, 4)),
            dma((N_PARTS, CHUNKS, 4)),
            dma((N_PARTS, CHUNKS, 4)),
            dma((4,)),
            dma((4,)),
        ],
        compiler_params=pltpu.CompilerParams(
            collective_id=0, has_side_effects=True, vmem_limit_bytes=60 * 2**20
        ),
        name="conv_and_score",
    )(
        tile_src[0].T,
        paper_feat.T,
        author_feat.T,
        weights,
        tile_col[0],
        relation.reshape(6, 128),
        send_rows[0],
        cand_send[0],
        neg_rows,
        cand_author.reshape(8, 128),
    )
    def hand_over(out_in, loss_in, out_to, loss_to):
        out_to[...] = out_in[...]
        loss_to[...] = loss_in[...]

    out, loss = pl.pallas_call(
        hand_over,
        out_shape=(
            jax.ShapeDtypeStruct((W, ROWS), BF),
            jax.ShapeDtypeStruct((8, 128), F32),
        ),
        in_specs=[vmem, vmem],
        out_specs=(vmem, vmem),
        name="hand_over",
    )(out, loss)
    return out.T, loss.reshape(-1)


def solution(mesh):
    placed = (
        P("owner", "rep"),
        P("owner", "rep"),
        P(),
        P(),
        P("owner", None, None),
        P(None, None, "owner"),
        P(None, None, "owner"),
        P("owner"),
        P("owner", None, None),
        P("owner", None),
    )
    return jax.shard_map(
        per_device,
        mesh=mesh,
        in_specs=placed,
        out_specs=(P("owner", "rep"), P("owner")),
        check_vma=False,
    )
```
